128 devices in a mesh: dp: 4 (over y), mem: 32 (over x, z, core).
Axes of the slice: x: 4, y: 4, z: 4, core: 2. Of those that a mesh axis runs over, the one named last changes fastest.
Arguments:
- images: bfloat16 [256, 577, 768], P(('dp', 'mem')), may hold values from -300 to 300
- text_cache: bfloat16 [2048, 40, 768], P('mem'), may hold values from -50 to 50
- cand_ids: int32 [256, 16], P(('dp', 'mem')), may hold values from 0 to 2047, as said below
- cand_slot: int32 [256, 16], P(('dp', 'mem')), may hold values from 0 to 15, each once within a row
- w_query: bfloat16 [768, 768], replicated, may hold values from -0.21875 to 0.21875
- w_key: bfloat16 [768, 768], replicated, may hold values from -0.21875 to 0.21875
- w_value: bfloat16 [768, 768], replicated, may hold values from -0.21875 to 0.21875
- w_out: bfloat16 [768, 768], replicated, may hold values from -0.21875 to 0.21875
- out_bias: float32 [768], replicated, may hold values from -3 to 3
- norm1_gain: float32 [768], replicated, may hold values from 0.5 to 1.5
- norm1_shift: float32 [768], replicated, may hold values from -1.8 to 1.8
- w_up: bfloat16 [768, 3072], replicated, may hold values from -0.21875 to 0.21875
- up_bias: float32 [3072], replicated, may hold values from -3 to 3
- w_down: bfloat16 [3072, 768], replicated, may hold values from -0.109375 to 0.109375
- down_bias: float32 [768], replicated, may hold values from -3 to 3
- norm2_gain: float32 [768], replicated, may hold values from 0.5 to 1.5
- norm2_shift: float32 [768], replicated, may hold values from -1.8 to 1.8
Outputs:
- pair_states: bfloat16 [4096, 40, 768], P(('dp', 'mem'))
The draws below stay inside these ranges and needn't reach their ends.
Inputs may be any that keep to these rules, and one draw needn't show every extreme that they name: `cand_ids`: in every device's block of 2 images (its 32 candidates), at most 2 candidates lie on one memory shard (ids s * 64 to (s + 1) * 64 - 1), and in every such block some shard holds exactly 2.
All inputs are finite; a program needn't handle non-finite values.
Results may differ from the reference program's by a relative error of at most 0.01.
The reference program's roundings to bfloat16 on the way count: a program that leaves them out, or rounds other values in their place, can miss the bound.
Values may be sent and summed in bfloat16 or wider, within the bound.
A program may use at most 192 MiB of HBM per device.

```python
import jax
import jax.numpy as jnp
from jax import lax

D = 768
HEADS = 12
FF = 3072
PATCHES = 577
WORDS = 40
CANDS = 16
IMG_DEV = 2
CAP_DEV = 64
HEAD_DIM = 64
GROUP_COUNT = 4
MEM_SHARDS = 32
CG = 4
IMAGES = 256
CAPTIONS = 2048
PAIRS = 4096
MOST = 2


def draw_images(key, part):
    key = jax.random.fold_in(key, 11)
    k_base = jax.random.fold_in(key, 0)
    panel_shape = (IMAGES, PATCHES, D)
    values = jax.random.truncated_normal(k_base, -5.0, 5.0, panel_shape, jnp.float32)
    return values.astype(jnp.bfloat16)


def draw_text_cache(key, part):
    key = jax.random.fold_in(key, 5)
    k_base, k_rows, k_cols = jax.random.split(key, 3)
    cache_shape = (CAPTIONS, WORDS, D)
    row_scale = jnp.exp(jax.random.uniform(k_rows, (CAPTIONS, WORDS, 1), jnp.float32, jnp.log(0.3), jnp.log(3.0)))
    col_scale = jnp.exp(jax.random.uniform(k_cols, (1, 1, D), jnp.float32, jnp.log(0.3), jnp.log(3.0)))
    base_vals = jax.random.truncated_normal(k_base, -5.0, 5.0, cache_shape, jnp.float32)
    return (base_vals * row_scale * col_scale).astype(jnp.bfloat16)


def draw_cand_ids(key, part):
    key = jax.random.fold_in(key, 7)
    k_popular, k_hot, k_turn, k_order, k_within = jax.random.split(key, 5)
    shard_count = CAPTIONS // CAP_DEV
    block_rows = IMG_DEV * CANDS
    block_count = IMAGES // IMG_DEV
    popular_count = max(1, shard_count // 8)
    popular = jax.random.permutation(k_popular, shard_count)[:popular_count]
    hot_shard = popular[jax.random.randint(k_hot, (block_count,), 0, popular_count)]
    turn_by = jax.random.randint(k_turn, (block_count, 1), 0, shard_count - 1)
    place_ids = jnp.arange(block_rows, dtype=jnp.int32)[None, :]
    others = (hot_shard[:, None] + 1 + (place_ids - MOST + turn_by) % (shard_count - 1)) % shard_count
    owners = jnp.where(place_ids < MOST, hot_shard[:, None], others)
    order_keys = jax.random.split(k_order, block_count)
    orders = jax.vmap(lambda one_key: jax.random.permutation(one_key, block_rows))(order_keys)
    owners = jnp.take_along_axis(owners, orders, axis=1)
    within_shard = jax.random.randint(k_within, (block_count, block_rows), 0, CAP_DEV)
    return (owners * CAP_DEV + within_shard).reshape(IMAGES, CANDS).astype(jnp.int32)


def bell_draw(key, extent, scale, most, kind=jnp.bfloat16):
    result = jax.random.normal(key, extent, jnp.float32) * scale
    return jnp.minimum(jnp.maximum(result, -most), most).astype(kind)


def setup_inputs(seed: int = 0) -> dict:
    keys = jax.random.split(jax.random.key(seed), 18)
    return {
        "images": draw_images(jax.random.fold_in(keys[17], 71), 0),
        "text_cache": draw_text_cache(jax.random.fold_in(keys[17], 71), 0),
        "cand_ids": draw_cand_ids(jax.random.fold_in(keys[17], 71), 0),
        "cand_slot": jax.vmap(lambda own: jax.random.permutation(own, CANDS))(jax.random.split(keys[3], IMAGES)).reshape((IMAGES, CANDS)).astype(jnp.int32),
        "w_query": bell_draw(keys[4], (D, D), D ** -0.5, 0.21875),
        "w_key": bell_draw(keys[5], (D, D), D ** -0.5, 0.21875),
        "w_value": bell_draw(keys[6], (D, D), D ** -0.5, 0.21875),
        "w_out": bell_draw(keys[7], (D, D), D ** -0.5, 0.21875),
        "out_bias": bell_draw(keys[8], (D,), 0.5, 3.0, jnp.float32),
        "norm1_gain": jnp.clip(1.0 + 0.1 * jax.random.normal(keys[9], (D,), jnp.float32), 0.5, 1.5),
        "norm1_shift": bell_draw(keys[10], (D,), 0.3, 1.8, jnp.float32),
        "w_up": bell_draw(keys[11], (D, FF), D ** -0.5, 0.21875),
        "up_bias": bell_draw(keys[12], (FF,), 0.5, 3.0, jnp.float32),
        "w_down": bell_draw(keys[13], (FF, D), FF ** -0.5, 0.109375),
        "down_bias": bell_draw(keys[14], (D,), 0.5, 3.0, jnp.float32),
        "norm2_gain": jnp.clip(1.0 + 0.1 * jax.random.normal(keys[15], (D,), jnp.float32), 0.5, 1.5),
        "norm2_shift": bell_draw(keys[16], (D,), 0.3, 1.8, jnp.float32),
    }


NORM_EPS = 1e-06

def normalize(values, gain, shift):
    center = values - lax.optimization_barrier(jnp.mean(values, axis=-1, keepdims=True))
    spread = lax.optimization_barrier(jnp.mean(center * center, axis=-1, keepdims=True))
    return center * lax.rsqrt(spread + NORM_EPS) * gain + shift

def encode_image(text_rows, key_rows, value_rows, w_query, w_out, out_bias, norm1_gain, norm1_shift, w_up, up_bias, w_down, down_bias, norm2_gain, norm2_shift):
    row_count = text_rows.shape[0]
    queries = jnp.dot(text_rows, w_query, preferred_element_type=jnp.float32).astype(jnp.bfloat16)
    q_heads = queries.reshape(row_count, HEADS, HEAD_DIM).astype(jnp.float32)
    k_heads = key_rows.reshape(PATCHES, HEADS, HEAD_DIM).astype(jnp.float32)
    v_heads = value_rows.reshape(PATCHES, HEADS, HEAD_DIM).astype(jnp.float32)
    scores = jnp.einsum('rhc,phc->hrp', q_heads, k_heads) * HEAD_DIM ** (-0.5)
    row_max = lax.optimization_barrier(jnp.max(scores, axis=-1, keepdims=True))
    exp_terms = jnp.exp(scores - row_max)
    attn_probs = (exp_terms / lax.optimization_barrier(jnp.sum(exp_terms, axis=-1, keepdims=True))).astype(jnp.bfloat16)
    context = jnp.einsum('hrp,phc->rhc', attn_probs.astype(jnp.float32), v_heads).astype(jnp.bfloat16)
    attended = jnp.dot(context.reshape(row_count, D), w_out, preferred_element_type=jnp.float32)
    first_out = normalize(attended + out_bias + text_rows.astype(jnp.float32), norm1_gain, norm1_shift).astype(jnp.bfloat16)
    hidden = jax.nn.gelu(jnp.dot(first_out, w_up, preferred_element_type=jnp.float32) + up_bias, approximate=False).astype(jnp.bfloat16)
    output = jnp.dot(hidden, w_down, preferred_element_type=jnp.float32) + down_bias + first_out.astype(jnp.float32)
    return normalize(output, norm2_gain, norm2_shift).astype(jnp.bfloat16)

def reference(images, text_cache, cand_ids, cand_slot, w_query, w_key, w_value, w_out, out_bias, norm1_gain, norm1_shift, w_up, up_bias, w_down, down_bias, norm2_gain, norm2_shift):

    def per_image(inputs):
        panel, caption_ids = inputs
        key_rows = jnp.dot(panel, w_key, preferred_element_type=jnp.float32).astype(jnp.bfloat16)
        value_rows = jnp.dot(panel, w_value, preferred_element_type=jnp.float32).astype(jnp.bfloat16)
        text_rows = jnp.take(text_cache, caption_ids, axis=0).reshape(CANDS * WORDS, D)
        return encode_image(text_rows, key_rows, value_rows, w_query, w_out, out_bias, norm1_gain, norm1_shift, w_up, up_bias, w_down, down_bias, norm2_gain, norm2_shift)
    states = lax.map(per_image, (images, cand_ids))
    image_index = jnp.arange(IMAGES, dtype=jnp.int32)
    source_row = image_index // (IMG_DEV * MEM_SHARDS)
    shard_index = image_index // IMG_DEV % MEM_SHARDS
    within_dev = image_index % IMG_DEV
    group_of = cand_slot // CG
    place_of = cand_slot % CG
    dest_rows = ((group_of * MEM_SHARDS + shard_index[:, None]) * GROUP_COUNT + source_row[:, None]) * (IMG_DEV * CG) + within_dev[:, None] * CG + place_of
    placed = jnp.zeros((PAIRS, WORDS, D), jnp.bfloat16)
    return placed.at[dest_rows.reshape(-1).astype(jnp.int32)].set(states.reshape(PAIRS, WORDS, D))
```

```python
import functools
import math

import jax
import jax.numpy as jnp
from jax import lax
from jax.experimental import pallas as pl
from jax.experimental.pallas import tpu as pltpu
from jax.sharding import PartitionSpec as P

MESH = pl.DeviceIdType.MESH
F32 = jnp.float32
BF16 = jnp.bfloat16
HEADS = 12
NORM_EPS = 1e-06
PIECE = 8
SLOTS = 2
LANES = 128
NT = (((1,), (1,)), ((), ()))


def normalize(values, gain, shift):
    center = values - jnp.mean(values, axis=-1, keepdims=True)
    spread = jnp.mean(center * center, axis=-1, keepdims=True)
    return center * lax.rsqrt(spread + NORM_EPS) * gain + shift


def project_images(img, w_key, w_value, keys, values_t):
    images, patches, width = img.shape
    whole = patches // 16 * 16
    rest = patches - whole
    for t in range(images):
        panel = img[t]
        rows = jnp.dot(panel, w_key[...], preferred_element_type=F32)
        keys[t, 0:whole, :] = rows[0:whole].astype(BF16)
        tail = jnp.concatenate([rows[whole:patches], jnp.zeros((16 - rest, width), F32)], axis=0)
        keys[t, whole : whole + 16, :] = tail.astype(BF16)
        for col in range(0, width, LANES):
            part = jnp.dot(panel, w_value[:, col : col + LANES], preferred_element_type=F32)
            pad = jnp.zeros((values_t.shape[2] - patches, LANES), F32)
            values_t[t, col : col + LANES, :] = jnp.concatenate([part, pad], axis=0).T.astype(BF16)


def head_pair_scores(queries, keys, t, col, rows):
    both = queries[t * rows : (t + 1) * rows, col : col + LANES].astype(F32)
    first = lax.broadcasted_iota(jnp.int32, both.shape, 1) < LANES // 2
    stacked = jnp.concatenate([jnp.where(first, both, 0.0), jnp.where(first, 0.0, both)], axis=0)
    return lax.dot_general(
        keys[t, :, col : col + LANES], stacked.astype(BF16), NT, preferred_element_type=F32
    )


def exponentials(scores, patches, scale):
    whole = patches // 16 * 16
    body, tail = scores[0:whole], scores[whole:]
    row = lax.broadcasted_iota(jnp.int32, tail.shape, 0)
    tail = jnp.where(row < patches - whole, tail, -1e30)
    top = jnp.maximum(
        jnp.max(body, axis=0, keepdims=True), jnp.max(tail, axis=0, keepdims=True)
    )
    factor = scale * math.log2(math.e)
    body = jnp.exp2((body - top) * factor)
    tail = jnp.exp2((tail - top) * factor)
    total = jnp.sum(body, axis=0, keepdims=True) + jnp.sum(tail, axis=0, keepdims=True)
    return jnp.concatenate([body, tail], axis=0).astype(BF16), total


def attend(queries, keys, values_t, context, patches):
    images, padded, width = keys.shape
    rows = queries.shape[0] // images
    half = LANES // 2
    scale = (width // HEADS) ** (-0.5)
    order = [(t, col) for t in range(images) for col in range(0, width, LANES)]
    scores = head_pair_scores(queries, keys, *order[0], rows)
    for index, (t, col) in enumerate(order):
        following = None
        if index + 1 < len(order):
            following = head_pair_scores(queries, keys, *order[index + 1], rows)
        probs, total = exponentials(scores, patches, scale)
        mixed = jnp.dot(
            values_t[t, col : col + LANES, 0:padded], probs, preferred_element_type=F32
        )
        inverse = 1.0 / total
        mixed = jnp.concatenate(
            [
                mixed[0:half, 0:rows] * inverse[:, 0:rows],
                mixed[half:LANES, rows:] * inverse[:, rows:],
            ],
            axis=0,
        )
        context[t * rows : (t + 1) * rows, col : col + LANES] = mixed.T.astype(BF16)
        scores = following


def kernel(
    mem_size,
    dp_size,
    requests,
    targets,
    out_bias,
    gain1,
    shift1,
    up_bias,
    down_bias,
    gain2,
    shift2,
    cache_hbm,
    img_hbm,
    w_key_hbm,
    w_value_hbm,
    w_query_hbm,
    w_out_hbm,
    w_up_hbm,
    w_down_hbm,
    arrived_out,
    cache,
    img,
    w_key,
    w_value,
    w_query,
    w_out,
    w_up,
    w_down,
    wanted,
    wanted_smem,
    outgoing,
    incoming,
    select,
    keys,
    values_t,
    context,
    finished,
    local_sem,
    smem_sem,
    ask_send,
    ask_recv,
    text_send,
    text_recv,
    out_send,
    out_recv,
    own_sem,
):
    dp = lax.axis_index("dp")
    mem = lax.axis_index("mem")
    words = cache.shape[1]
    piece_count = words // PIECE
    patches = img.shape[1]
    images = img.shape[0]

    loads = [
        pltpu.make_async_copy(source, target, local_sem.at[index])
        for index, (source, target) in enumerate(
            [
                (cache_hbm, cache),
                (img_hbm, img),
                (w_key_hbm, w_key),
                (w_value_hbm, w_value),
                (w_query_hbm, w_query),
                (w_out_hbm, w_out),
                (w_up_hbm, w_up),
                (w_down_hbm, w_down),
            ]
        )
    ]
    for load in loads:
        load.start()

    barrier = pltpu.get_barrier_semaphore()

    def greet(step, carry):
        peer = lax.rem(mem + step, mem_size)
        pl.semaphore_signal(barrier, inc=1, device_id=(dp, peer), device_id_type=MESH)
        return carry

    lax.fori_loop(1, mem_size, greet, 0)
    for step in range(1, dp_size):
        pl.semaphore_signal(
            barrier, inc=1, device_id=(lax.rem(dp + step, dp_size), mem), device_id_type=MESH
        )
    pl.semaphore_wait(barrier, mem_size - 1 + dp_size - 1)

    def ask(step, carry):
        peer = lax.rem(mem + step, mem_size)
        pltpu.make_async_remote_copy(
            src_ref=requests.at[peer],
            dst_ref=wanted.at[mem],
            send_sem=ask_send,
            recv_sem=ask_recv,
            device_id=(dp, peer),
            device_id_type=MESH,
        ).start()
        return carry

    lax.fori_loop(1, mem_size, ask, 0)
    wanted[mem] = requests[mem]

    row_targets = targets[...]
    for col in range(0, select.shape[1], LANES):
        lane = lax.broadcasted_iota(jnp.int32, row_targets.shape, 1) + col
        select[:, col : col + LANES] = jnp.where(row_targets == lane, 1.0, 0.0).astype(BF16)

    others = pl.ds(0, mem_size - 1)
    pltpu.make_async_copy(wanted.at[others], wanted.at[others], ask_recv).wait()
    to_smem = pltpu.make_async_copy(wanted, wanted_smem, smem_sem)
    to_smem.start()
    loads[0].wait()
    to_smem.wait()

    def rows_for(peer, start):
        parts = [
            cache[wanted_smem[peer, 0, slot], start : start + PIECE, :].astype(F32)
            for slot in range(SLOTS)
        ]
        return jnp.concatenate(parts, axis=0).astype(BF16)

    for piece in range(piece_count):
        incoming[piece, mem] = rows_for(mem, piece * PIECE)

        def serve(step, carry, piece=piece):
            peer = lax.rem(mem + step, mem_size)
            outgoing[piece, peer] = rows_for(peer, piece * PIECE)
            pltpu.make_async_remote_copy(
                src_ref=outgoing.at[piece, peer],
                dst_ref=incoming.at[piece, mem],
                send_sem=text_send.at[piece],
                recv_sem=text_recv.at[piece],
                device_id=(dp, peer),
                device_id_type=MESH,
            ).start()
            return carry

        lax.fori_loop(1, mem_size, serve, 0)

    for load in loads[1:4]:
        load.wait()
    project_images(img, w_key, w_value, keys, values_t)
    for load in loads[4:]:
        load.wait()

    group_rows = finished.shape[2]
    half_rows = group_rows // images

    def work(piece, carry):
        pltpu.make_async_copy(
            incoming.at[piece, others], incoming.at[piece, others], text_recv.at[piece]
        ).wait()
        arrived = incoming[piece].reshape(-1, incoming.shape[3])
        text = jnp.dot(select[...], arrived, preferred_element_type=F32)
        text_rows = text.astype(BF16)
        queries = jnp.dot(text_rows, w_query[...], preferred_element_type=F32).astype(BF16)
        attend(queries, keys, values_t, context, patches)
        attended = jnp.dot(context[...], w_out[...], preferred_element_type=F32)
        first_out = normalize(
            attended + out_bias[...] + text_rows.astype(F32), gain1[...], shift1[...]
        ).astype(BF16)
        hidden = jnp.dot(first_out, w_up[...], preferred_element_type=F32) + up_bias[...]
        hidden = (0.5 * hidden * (1.0 + lax.erf(hidden * 0.5**0.5))).astype(BF16)
        output = jnp.dot(hidden, w_down[...], preferred_element_type=F32)
        output = output + down_bias[...] + first_out.astype(F32)
        encoded = normalize(output, gain2[...], shift2[...]).astype(BF16)
        for t in range(images):
            for group in range(dp_size):
                start = (t * dp_size + group) * half_rows
                finished[piece, group, t * half_rows : (t + 1) * half_rows, :] = encoded[
                    start : start + half_rows
                ]
        for step in range(1, dp_size):
            peer = lax.rem(dp + step, dp_size)
            pltpu.make_async_remote_copy(
                src_ref=finished.at[piece, peer],
                dst_ref=arrived_out.at[piece, dp],
                send_sem=out_send,
                recv_sem=out_recv,
                device_id=(peer, mem),
                device_id_type=MESH,
            ).start()
        pltpu.make_async_copy(
            finished.at[piece, dp], arrived_out.at[piece, dp], own_sem
        ).start()
        return carry

    lax.fori_loop(0, piece_count, work, 0)

    pltpu.make_async_copy(requests.at[others], requests.at[others], ask_send).wait()

    def drain(piece, carry):
        pltpu.make_async_copy(
            outgoing.at[piece, others], outgoing.at[piece, others], text_send.at[piece]
        ).wait()
        return carry

    lax.fori_loop(0, piece_count, drain, 0)
    sent = finished.at[:, pl.ds(0, dp_size - 1)]
    pltpu.make_async_copy(sent, sent, out_send).wait()
    came = arrived_out.at[:, pl.ds(0, dp_size - 1)]
    pltpu.make_async_copy(came, came, out_recv).wait()
    own = arrived_out.at[:, pl.ds(0, 1)]
    pltpu.make_async_copy(own, own, own_sem).wait()


def on_device(
    images,
    text_cache,
    cand_ids,
    cand_slot,
    w_query,
    w_key,
    w_value,
    w_out,
    out_bias,
    norm1_gain,
    norm1_shift,
    w_up,
    up_bias,
    w_down,
    down_bias,
    norm2_gain,
    norm2_shift,
):
    mem_size = lax.axis_size("mem")
    dp_size = lax.axis_size("dp")
    img_local, cand_count = cand_ids.shape
    cap_local, word_count, width = text_cache.shape
    patches = images.shape[1]
    hidden_width = w_up.shape[1]
    pair_count = img_local * cand_count
    piece_count = word_count // PIECE
    piece_rows = pair_count * PIECE
    slot_rows = SLOTS * PIECE
    padded = -(-patches // 16) * 16
    padded_lanes = -(-patches // LANES) * LANES

    flat_ids = cand_ids.reshape(pair_count)
    owner_of = flat_ids // cap_local
    local_row = flat_ids % cap_local
    position = jnp.arange(pair_count, dtype=jnp.int32)
    same_owner = (owner_of[:, None] == owner_of[None, :]) & (position[None, :] < position[:, None])
    owner_rank = jnp.sum(same_owner.astype(jnp.int32), axis=1)
    slot_index = owner_of * SLOTS + owner_rank
    table_slots = (
        jnp.arange(mem_size, dtype=jnp.int32)[:, None] * SLOTS
        + jnp.arange(LANES, dtype=jnp.int32)[None, :]
    )
    table_slots = jnp.where(jnp.arange(LANES)[None, :] < SLOTS, table_slots, -1)
    requests = jnp.sum(
        jnp.where(slot_index[None, None, :] == table_slots[:, :, None], local_row, 0), axis=2
    ).reshape(mem_size, 1, LANES)

    slot_ids = jnp.arange(cand_count, dtype=jnp.int32)
    matches = cand_slot[:, :, None] == slot_ids[None, None, :]
    slot_of = jnp.sum(
        jnp.where(matches, slot_index.reshape(img_local, cand_count, 1), 0), axis=1
    ).reshape(pair_count)
    targets = slot_of[:, None] * PIECE + jnp.arange(PIECE, dtype=jnp.int32)[None, :]
    targets = jnp.broadcast_to(targets.reshape(piece_rows, 1), (piece_rows, LANES))

    vmem = pl.BlockSpec(memory_space=pltpu.VMEM)
    anywhere = pl.BlockSpec(memory_space=pl.ANY)
    group_rows = piece_rows // dp_size
    result = pl.pallas_call(
        functools.partial(kernel, mem_size, dp_size),
        out_shape=jax.ShapeDtypeStruct((piece_count, dp_size, group_rows, width), BF16),
        in_specs=[vmem] * 9 + [anywhere] * 8,
        out_specs=anywhere,
        scratch_shapes=[
            pltpu.VMEM(text_cache.shape, BF16),
            pltpu.VMEM(images.shape, BF16),
            pltpu.VMEM((width, width), BF16),
            pltpu.VMEM((width, width), BF16),
            pltpu.VMEM((width, width), BF16),
            pltpu.VMEM((width, width), BF16),
            pltpu.VMEM((width, hidden_width), BF16),
            pltpu.VMEM((hidden_width, width), BF16),
            pltpu.VMEM((mem_size, 1, LANES), jnp.int32),
            pltpu.SMEM((mem_size, 1, LANES), jnp.int32),
            pltpu.VMEM((piece_count, mem_size, slot_rows, width), BF16),
            pltpu.VMEM((piece_count, mem_size, slot_rows, width), BF16),
            pltpu.VMEM((piece_rows, mem_size * slot_rows), BF16),
            pltpu.VMEM((img_local, padded, width), BF16),
            pltpu.VMEM((img_local, width, padded_lanes), BF16),
            pltpu.VMEM((piece_rows, width), BF16),
            pltpu.VMEM((piece_count, dp_size, group_rows, width), BF16),
            pltpu.SemaphoreType.DMA((8,)),
            pltpu.SemaphoreType.DMA,
            pltpu.SemaphoreType.DMA,
            pltpu.SemaphoreType.DMA,
            pltpu.SemaphoreType.DMA((piece_count,)),
            pltpu.SemaphoreType.DMA((piece_count,)),
            pltpu.SemaphoreType.DMA,
            pltpu.SemaphoreType.DMA,
            pltpu.SemaphoreType.DMA,
        ],
        compiler_params=pltpu.CompilerParams(
            collective_id=0, has_side_effects=True, vmem_limit_bytes=60 * 2**20
        ),
    )(
        requests,
        targets,
        out_bias.reshape(1, width),
        norm1_gain.reshape(1, width),
        norm1_shift.reshape(1, width),
        up_bias.reshape(1, hidden_width),
        down_bias.reshape(1, width),
        norm2_gain.reshape(1, width),
        norm2_shift.reshape(1, width),
        text_cache,
        images,
        w_key,
        w_value,
        w_query,
        w_out,
        w_up,
        w_down,
    )
    pairs = pair_count // dp_size
    result = result.reshape(piece_count, dp_size, pairs, PIECE, width)
    return result.transpose(1, 2, 0, 3, 4).reshape(pair_count, word_count, width)


def solution(mesh):
    split = P(("dp", "mem"), None, None)
    ids = P(("dp", "mem"), None)
    in_specs = (split, P("mem", None, None), ids, ids) + (P(),) * 13
    return jax.shard_map(
        on_device, mesh=mesh, in_specs=in_specs, out_specs=split, check_vma=False
    )
```

```python
import functools
import math

import jax
import jax.numpy as jnp
from jax import lax
from jax.experimental import pallas as pl
from jax.experimental.pallas import tpu as pltpu
from jax.sharding import PartitionSpec as P

MESH = pl.DeviceIdType.MESH
F32 = jnp.float32
BF16 = jnp.bfloat16
HEADS = 12
NORM_EPS = 1e-06
PIECE = 8
SLOTS = 2
LANES = 128
NT = (((1,), (1,)), ((), ()))


def normalize(values, gain, shift):
    center = values - jnp.mean(values, axis=-1, keepdims=True)
    spread = jnp.mean(center * center, axis=-1, keepdims=True)
    return center * lax.rsqrt(spread + NORM_EPS) * gain + shift


def project_images(img, w_key, w_value, keys, values_t, wide):
    patches, images, width = img.shape
    whole = patches // 16 * 16
    rest = patches - whole
    body = img[0:whole].reshape(whole * images, width)
    tail = img[whole:patches].reshape(rest * images, width)
    tail_rows = jnp.concatenate(
        [tail.astype(F32), jnp.zeros((16 - rest * images, width), F32)], axis=0
    ).astype(BF16)
    for weight, is_key in ((w_key, True), (w_value, False)):
        for col in range(0, width, 2 * LANES):
            double = slice(col, col + 2 * LANES)
            product = jnp.dot(body, weight[:, double], preferred_element_type=F32)
            last = jnp.dot(tail_rows, weight[:, double], preferred_element_type=F32)
            for side in range(2):
                here = slice(side * LANES, (side + 1) * LANES)
                cols = slice(col + side * LANES, col + (side + 1) * LANES)
                wide[side] = product[:, here]
                for t in range(images):
                    rows = wide[side, pl.ds(t, whole, stride=images), :]
                    ends = [last[t + images * p : t + images * p + 1, here] for p in range(rest)]
                    if is_key:
                        ends.append(jnp.zeros((16 - rest, LANES), F32))
                        keys[t, 0:whole, cols] = rows.astype(BF16)
                        keys[t, whole : whole + 16, cols] = jnp.concatenate(ends, 0).astype(BF16)
                    else:
                        pad = jnp.zeros((values_t.shape[2] - patches, LANES), F32)
                        rows = jnp.concatenate([rows, *ends, pad], axis=0)
                        values_t[t, cols, :] = rows.T.astype(BF16)


def spread_lanes(ref):
    return jnp.concatenate([ref[row : row + 1, :] for row in range(ref.shape[0])], axis=1)


def plan(cand_ids, cand_slot, requests, select, cap_local):
    mem_size = requests.shape[0]
    images, cands = cand_ids.shape
    pairs = [(t, j) for t in range(images) for j in range(cands)]
    owners = [lax.div(cand_ids[t, j], cap_local) for t, j in pairs]
    rows = [lax.rem(cand_ids[t, j], cap_local) for t, j in pairs]
    shape = (max(mem_size, len(pairs)), LANES)
    sub = lax.broadcasted_iota(jnp.int32, shape, 0)
    lane = lax.broadcasted_iota(jnp.int32, shape, 1)
    slot_key = jnp.where(lane < SLOTS, sub * SLOTS + lane, -1)
    table = jnp.zeros(shape, jnp.int32)
    slot_of = jnp.zeros(shape, jnp.int32)
    for n, (t, j) in enumerate(pairs):
        slot = owners[n] * SLOTS
        for before in range(n):
            slot = slot + jnp.where(owners[before] == owners[n], 1, 0)
        table = jnp.where(slot_key == slot, rows[n], table)
        slot_of = jnp.where(sub == t * cands + cand_slot[t, j], slot, slot_of)
    for shard in range(mem_size):
        requests[shard] = table[shard : shard + 1, :]
    word = lax.broadcasted_iota(jnp.int32, (PIECE, LANES), 0)
    wanted_rows = jnp.concatenate(
        [
            jnp.broadcast_to(slot_of[n : n + 1, :], (PIECE, LANES)) * PIECE + word
            for n in range(len(pairs))
        ],
        axis=0,
    )
    for col in range(0, select.shape[1], LANES):
        here = lax.broadcasted_iota(jnp.int32, wanted_rows.shape, 1) + col
        select[:, col : col + LANES] = jnp.where(wanted_rows == here, 1.0, 0.0).astype(BF16)


def head_pair_scores(queries, keys, t, col, rows):
    both = queries[t * rows : (t + 1) * rows, col : col + LANES].astype(F32)
    first = lax.broadcasted_iota(jnp.int32, both.shape, 1) < LANES // 2
    stacked = jnp.concatenate([jnp.where(first, both, 0.0), jnp.where(first, 0.0, both)], axis=0)
    return lax.dot_general(
        keys[t, :, col : col + LANES], stacked.astype(BF16), NT, preferred_element_type=F32
    )


def exponentials(scores, patches, scale):
    whole = patches // 16 * 16
    body, tail = scores[0:whole], scores[whole:]
    row = lax.broadcasted_iota(jnp.int32, tail.shape, 0)
    tail = jnp.where(row < patches - whole, tail, -1e30)
    top = jnp.maximum(
        jnp.max(body, axis=0, keepdims=True), jnp.max(tail, axis=0, keepdims=True)
    )
    factor = scale * math.log2(math.e)
    body = jnp.exp2((body - top) * factor)
    tail = jnp.exp2((tail - top) * factor)
    total = jnp.sum(body, axis=0, keepdims=True) + jnp.sum(tail, axis=0, keepdims=True)
    return jnp.concatenate([body, tail], axis=0).astype(BF16), total


def attend(queries, keys, values_t, context, patches):
    images, padded, width = keys.shape
    rows = queries.shape[0] // images
    half = LANES // 2
    scale = (width // HEADS) ** (-0.5)
    order = [(t, col) for t in range(images) for col in range(0, width, LANES)]
    scores = head_pair_scores(queries, keys, *order[0], rows)
    for index, (t, col) in enumerate(order):
        following = None
        if index + 1 < len(order):
            following = head_pair_scores(queries, keys, *order[index + 1], rows)
        probs, total = exponentials(scores, patches, scale)
        mixed = jnp.dot(
            values_t[t, col : col + LANES, 0:padded], probs, preferred_element_type=F32
        )
        inverse = 1.0 / total
        mixed = jnp.concatenate(
            [
                mixed[0:half, 0:rows] * inverse[:, 0:rows],
                mixed[half:LANES, rows:] * inverse[:, rows:],
            ],
            axis=0,
        )
        context[t * rows : (t + 1) * rows, col : col + LANES] = mixed.T.astype(BF16)
        scores = following


def kernel(
    mem_size,
    dp_size,
    cand_ids,
    cand_slot,
    out_bias,
    gain1,
    shift1,
    up_bias,
    down_bias,
    gain2,
    shift2,
    cache_hbm,
    img_hbm,
    w_key_hbm,
    w_value_hbm,
    w_query_hbm,
    w_out_hbm,
    w_up_hbm,
    w_down_hbm,
    arrived_out,
    cache,
    img,
    w_key,
    w_value,
    w_query,
    w_out,
    w_up,
    w_down,
    wide,
    requests,
    wanted,
    wanted_smem,
    outgoing,
    incoming,
    select,
    keys,
    values_t,
    context,
    finished,
    local_sem,
    smem_sem,
    ask_send,
    ask_recv,
    text_send,
    text_recv,
    out_send,
    out_recv,
    own_sem,
):
    dp = lax.axis_index("dp")
    mem = lax.axis_index("mem")
    words = cache.shape[1]
    piece_count = words // PIECE
    patches, images = img.shape[0:2]

    loads = [
        pltpu.make_async_copy(source, target, local_sem.at[index])
        for index, (source, target) in enumerate(
            [
                (cache_hbm, cache),
                (img_hbm, img),
                (w_key_hbm, w_key),
                (w_value_hbm, w_value),
                (w_query_hbm, w_query),
                (w_out_hbm, w_out),
                (w_up_hbm, w_up),
                (w_down_hbm, w_down),
            ]
        )
    ]
    for load in loads:
        load.start()

    barrier = pltpu.get_barrier_semaphore()

    def greet(step, carry):
        peer = lax.rem(mem + step, mem_size)
        pl.semaphore_signal(barrier, inc=1, device_id=(dp, peer), device_id_type=MESH)
        return carry

    lax.fori_loop(1, mem_size, greet, 0)
    for step in range(1, dp_size):
        pl.semaphore_signal(
            barrier, inc=1, device_id=(lax.rem(dp + step, dp_size), mem), device_id_type=MESH
        )
    plan(cand_ids, cand_slot, requests, select, cache.shape[0])
    pl.semaphore_wait(barrier, mem_size - 1 + dp_size - 1)

    def ask(step, carry):
        peer = lax.rem(mem + step, mem_size)
        pltpu.make_async_remote_copy(
            src_ref=requests.at[peer],
            dst_ref=wanted.at[mem],
            send_sem=ask_send,
            recv_sem=ask_recv,
            device_id=(dp, peer),
            device_id_type=MESH,
        ).start()
        return carry

    lax.fori_loop(1, mem_size, ask, 0)
    wanted[mem] = requests[mem]

    others = pl.ds(0, mem_size - 1)
    pltpu.make_async_copy(wanted.at[others], wanted.at[others], ask_recv).wait()
    to_smem = pltpu.make_async_copy(wanted, wanted_smem, smem_sem)
    to_smem.start()
    loads[0].wait()
    to_smem.wait()

    def rows_for(peer, start):
        parts = [
            cache[wanted_smem[peer, 0, slot], start : start + PIECE, :].astype(F32)
            for slot in range(SLOTS)
        ]
        return jnp.concatenate(parts, axis=0).astype(BF16)

    for piece in range(piece_count):
        incoming[piece, mem] = rows_for(mem, piece * PIECE)

        def serve(step, carry, piece=piece):
            peer = lax.rem(mem + lax.rem(step * 13, mem_size), mem_size)
            outgoing[piece, peer] = rows_for(peer, piece * PIECE)
            pltpu.make_async_remote_copy(
                src_ref=outgoing.at[piece, peer],
                dst_ref=incoming.at[piece, mem],
                send_sem=text_send.at[piece],
                recv_sem=text_recv.at[piece],
                device_id=(dp, peer),
                device_id_type=MESH,
            ).start()
            return carry

        lax.fori_loop(1, mem_size, serve, 0)

    for load in loads[1:4]:
        load.wait()
    project_images(img, w_key, w_value, keys, values_t, wide)
    for load in loads[4:]:
        load.wait()

    group_rows = finished.shape[2]
    half_rows = group_rows // images

    def work(piece, carry):
        pltpu.make_async_copy(
            incoming.at[piece, others], incoming.at[piece, others], text_recv.at[piece]
        ).wait()
        arrived = incoming[piece].reshape(-1, incoming.shape[3])
        text = jnp.dot(select[...], arrived, preferred_element_type=F32)
        text_rows = text.astype(BF16)
        queries = jnp.dot(text_rows, w_query[...], preferred_element_type=F32).astype(BF16)
        attend(queries, keys, values_t, context, patches)
        attended = jnp.dot(context[...], w_out[...], preferred_element_type=F32)
        first_out = normalize(
            attended + spread_lanes(out_bias) + text_rows.astype(F32), spread_lanes(gain1), spread_lanes(shift1)
        ).astype(BF16)
        hidden = jnp.dot(first_out, w_up[...], preferred_element_type=F32) + spread_lanes(up_bias)
        hidden = (0.5 * hidden * (1.0 + lax.erf(hidden * 0.5**0.5))).astype(BF16)
        output = jnp.dot(hidden, w_down[...], preferred_element_type=F32)
        output = output + spread_lanes(down_bias) + first_out.astype(F32)
        encoded = normalize(output, spread_lanes(gain2), spread_lanes(shift2)).astype(BF16)
        for t in range(images):
            for group in range(dp_size):
                start = (t * dp_size + group) * half_rows
                finished[piece, group, t * half_rows : (t + 1) * half_rows, :] = encoded[
                    start : start + half_rows
                ]
        for step in range(1, dp_size):
            peer = lax.rem(dp + step, dp_size)
            pltpu.make_async_remote_copy(
                src_ref=finished.at[piece, peer],
                dst_ref=arrived_out.at[piece, dp],
                send_sem=out_send,
                recv_sem=out_recv,
                device_id=(peer, mem),
                device_id_type=MESH,
            ).start()
        pltpu.make_async_copy(
            finished.at[piece, dp], arrived_out.at[piece, dp], own_sem
        ).start()
        return carry

    lax.fori_loop(0, piece_count, work, 0)

    pltpu.make_async_copy(requests.at[others], requests.at[others], ask_send).wait()

    def drain(piece, carry):
        pltpu.make_async_copy(
            outgoing.at[piece, others], outgoing.at[piece, others], text_send.at[piece]
        ).wait()
        return carry

    lax.fori_loop(0, piece_count, drain, 0)
    sent = finished.at[:, pl.ds(0, dp_size - 1)]
    pltpu.make_async_copy(sent, sent, out_send).wait()
    came = arrived_out.at[:, pl.ds(0, dp_size - 1)]
    pltpu.make_async_copy(came, came, out_recv).wait()
    own = arrived_out.at[:, pl.ds(0, 1)]
    pltpu.make_async_copy(own, own, own_sem).wait()


def on_device(
    images,
    text_cache,
    cand_ids,
    cand_slot,
    w_query,
    w_key,
    w_value,
    w_out,
    out_bias,
    norm1_gain,
    norm1_shift,
    w_up,
    up_bias,
    w_down,
    down_bias,
    norm2_gain,
    norm2_shift,
):
    mem_size = lax.axis_size("mem")
    dp_size = lax.axis_size("dp")
    img_local, cand_count = cand_ids.shape
    word_count, width = text_cache.shape[1:]
    patches = images.shape[1]
    hidden_width = w_up.shape[1]
    pair_count = img_local * cand_count
    piece_count = word_count // PIECE
    piece_rows = pair_count * PIECE
    slot_rows = SLOTS * PIECE
    padded = -(-patches // 16) * 16
    padded_lanes = -(-patches // LANES) * LANES

    vmem = pl.BlockSpec(memory_space=pltpu.VMEM)
    smem = pl.BlockSpec(memory_space=pltpu.SMEM)
    anywhere = pl.BlockSpec(memory_space=pl.ANY)
    group_rows = piece_rows // dp_size
    result = pl.pallas_call(
        functools.partial(kernel, mem_size, dp_size),
        out_shape=jax.ShapeDtypeStruct((piece_count, dp_size, group_rows, width), BF16),
        in_specs=[smem] * 2 + [vmem] * 7 + [anywhere] * 8,
        out_specs=anywhere,
        scratch_shapes=[
            pltpu.VMEM(text_cache.shape, BF16),
            pltpu.VMEM((patches, img_local, width), BF16),
            pltpu.VMEM((width, width), BF16),
            pltpu.VMEM((width, width), BF16),
            pltpu.VMEM((width, width), BF16),
            pltpu.VMEM((width, width), BF16),
            pltpu.VMEM((width, hidden_width), BF16),
            pltpu.VMEM((hidden_width, width), BF16),
            pltpu.VMEM((2, patches // 16 * 16 * img_local, LANES), F32),
            pltpu.VMEM((mem_size, 1, LANES), jnp.int32),
            pltpu.VMEM((mem_size, 1, LANES), jnp.int32),
            pltpu.SMEM((mem_size, 1, LANES), jnp.int32),
            pltpu.VMEM((piece_count, mem_size, slot_rows, width), BF16),
            pltpu.VMEM((piece_count, mem_size, slot_rows, width), BF16),
            pltpu.VMEM((piece_rows, mem_size * slot_rows), BF16),
            pltpu.VMEM((img_local, padded, width), BF16),
            pltpu.VMEM((img_local, width, padded_lanes), BF16),
            pltpu.VMEM((piece_rows, width), BF16),
            pltpu.VMEM((piece_count, dp_size, group_rows, width), BF16),
            pltpu.SemaphoreType.DMA((8,)),
            pltpu.SemaphoreType.DMA,
            pltpu.SemaphoreType.DMA,
            pltpu.SemaphoreType.DMA,
            pltpu.SemaphoreType.DMA((piece_count,)),
            pltpu.SemaphoreType.DMA((piece_count,)),
            pltpu.SemaphoreType.DMA,
            pltpu.SemaphoreType.DMA,
            pltpu.SemaphoreType.DMA,
        ],
        compiler_params=pltpu.CompilerParams(
            collective_id=0, has_side_effects=True, vmem_limit_bytes=60 * 2**20
        ),
    )(
        cand_ids,
        cand_slot,
        *(
            vector.reshape(-1, LANES)
            for vector in (
                out_bias,
                norm1_gain,
                norm1_shift,
                up_bias,
                down_bias,
                norm2_gain,
                norm2_shift,
            )
        ),
        text_cache,
        images.transpose(1, 0, 2),
        w_key,
        w_value,
        w_query,
        w_out,
        w_up,
        w_down,
    )
    pairs = pair_count // dp_size
    result = result.reshape(piece_count, dp_size, pairs, PIECE, width)
    return result.transpose(1, 2, 0, 3, 4).reshape(pair_count, word_count, width)


def solution(mesh):
    split = P(("dp", "mem"), None, None)
    ids = P(("dp", "mem"), None)
    in_specs = (split, P("mem", None, None), ids, ids) + (P(),) * 13
    return jax.shard_map(
        on_device, mesh=mesh, in_specs=in_specs, out_specs=split, check_vma=False
    )
```

```python
import functools
import math

import jax
import jax.numpy as jnp
from jax import lax
from jax.experimental import pallas as pl
from jax.experimental.pallas import tpu as pltpu
from jax.sharding import PartitionSpec as P

MESH = pl.DeviceIdType.MESH
F32 = jnp.float32
BF16 = jnp.bfloat16
HEADS = 12
NORM_EPS = 1e-06
PIECE = 4
PAIRED = 2
SLOTS = 2
LANES = 128
NT = (((1,), (1,)), ((), ()))


def normalize(values, gain, shift):
    center = values - jnp.mean(values, axis=-1, keepdims=True)
    spread = jnp.mean(center * center, axis=-1, keepdims=True)
    return center * lax.rsqrt(spread + NORM_EPS) * gain + shift


def project_images(img, weight, wide, store):
    patches, images, width = img.shape
    whole = patches // 16 * 16
    rest = patches - whole
    body = img[0:whole].reshape(whole * images, width)
    tail = img[whole:patches].reshape(rest * images, width)
    tail_rows = jnp.concatenate(
        [tail.astype(F32), jnp.zeros((16 - rest * images, width), F32)], axis=0
    ).astype(BF16)
    for col in range(0, width, 2 * LANES):
        double = slice(col, col + 2 * LANES)
        product = jnp.dot(body, weight[:, double], preferred_element_type=F32)
        last = jnp.dot(tail_rows, weight[:, double], preferred_element_type=F32)
        for side in range(2):
            here = slice(side * LANES, (side + 1) * LANES)
            wide[side] = product[:, here]
            for t in range(images):
                rows = wide[side, pl.ds(t, whole, stride=images), :]
                ends = [last[t + images * p : t + images * p + 1, here] for p in range(rest)]
                store(t, col + side * LANES, rows, ends)


def project_keys(img, w_key, keys, wide):
    def store(t, col, rows, ends):
        cols = slice(col, col + LANES)
        whole, rest = rows.shape[0], len(ends)
        ends = [*ends, jnp.zeros((16 - rest, LANES), F32)]
        keys[t, 0:whole, cols] = rows.astype(BF16)
        keys[t, whole : whole + 16, cols] = jnp.concatenate(ends, axis=0).astype(BF16)

    project_images(img, w_key, wide, store)


def project_values(img, w_value, values_t, wide):
    def store(t, col, rows, ends):
        pad = jnp.zeros((values_t.shape[2] - rows.shape[0] - len(ends), LANES), F32)
        rows = jnp.concatenate([rows, *ends, pad], axis=0)
        values_t[t, col : col + LANES, :] = rows.T.astype(BF16)

    project_images(img, w_value, wide, store)


def spread_lanes(ref):
    return jnp.concatenate([ref[row : row + 1, :] for row in range(ref.shape[0])], axis=1)


def plan(cand_ids, cand_slot, requests, select, cap_local):
    mem_size = requests.shape[0]
    images, cands = cand_ids.shape
    pairs = [(t, j) for t in range(images) for j in range(cands)]
    owners = [lax.div(cand_ids[t, j], cap_local) for t, j in pairs]
    rows = [lax.rem(cand_ids[t, j], cap_local) for t, j in pairs]
    shape = (max(mem_size, len(pairs)), LANES)
    sub = lax.broadcasted_iota(jnp.int32, shape, 0)
    lane = lax.broadcasted_iota(jnp.int32, shape, 1)
    slot_key = jnp.where(lane < SLOTS, sub * SLOTS + lane, -1)
    table = jnp.zeros(shape, jnp.int32)
    slot_of = jnp.zeros(shape, jnp.int32)
    for n, (t, j) in enumerate(pairs):
        slot = owners[n] * SLOTS
        for before in range(n):
            slot = slot + jnp.where(owners[before] == owners[n], 1, 0)
        table = jnp.where(slot_key == slot, rows[n], table)
        slot_of = jnp.where(sub == t * cands + cand_slot[t, j], slot, slot_of)
    for shard in range(mem_size):
        requests[shard] = table[shard : shard + 1, :]
    word = lax.broadcasted_iota(jnp.int32, (PIECE, LANES), 0)
    wanted_rows = jnp.concatenate(
        [
            jnp.broadcast_to(slot_of[n : n + 1, :], (PIECE, LANES)) * PIECE + word
            for n in range(len(pairs))
        ],
        axis=0,
    )
    for col in range(0, select.shape[1], LANES):
        here = lax.broadcasted_iota(jnp.int32, wanted_rows.shape, 1) + col
        select[:, col : col + LANES] = jnp.where(wanted_rows == here, 1.0, 0.0).astype(BF16)


def head_scores(queries, keys, t, col, rows, span, head_dim):
    these = queries[t * rows : (t + 1) * rows, col : col + span].astype(F32)
    head = lax.broadcasted_iota(jnp.int32, these.shape, 1) // head_dim
    stacked = jnp.concatenate(
        [jnp.where(head == h, these, 0.0) for h in range(span // head_dim)], axis=0
    )
    return lax.dot_general(
        keys[t, :, col : col + span], stacked.astype(BF16), NT, preferred_element_type=F32
    )


def exponentials(scores, patches, scale):
    whole = patches // 16 * 16
    tail = scores[whole:]
    row = lax.broadcasted_iota(jnp.int32, tail.shape, 0)
    tail = jnp.where(row < patches - whole, tail, -1e30)
    top = jnp.maximum(
        jnp.max(scores[0:whole], axis=0, keepdims=True), jnp.max(tail, axis=0, keepdims=True)
    )
    factor = scale * math.log2(math.e)
    parts, total = [], 0.0
    for start in range(0, whole + 16, 16):
        part = tail if start == whole else scores[start : start + 16]
        part = jnp.exp2((part - top) * factor)
        parts.append(part.astype(BF16))
        total = total + part
    return jnp.concatenate(parts, axis=0), jnp.sum(total, axis=0, keepdims=True)


def attend(queries, keys, values_t, context, patches):
    images, padded, width = keys.shape
    rows = queries.shape[0] // images
    head_dim = width // HEADS
    span = 2 * LANES // rows * head_dim
    scale = head_dim ** (-0.5)
    order = [(t, col) for t in range(images) for col in range(0, width, span)]
    scores = [head_scores(queries, keys, t, col, rows, span, head_dim) for t, col in order]
    probs = [exponentials(one, patches, scale) for one in scores]
    for (t, col), (one, total) in zip(order, probs):
        mixed = jnp.dot(values_t[t, col : col + span, 0:padded], one, preferred_element_type=F32)
        mixed = mixed * (1.0 / total)
        own = [
            mixed[h * head_dim : (h + 1) * head_dim, h * rows : (h + 1) * rows]
            for h in range(span // head_dim)
        ]
        context[t * rows : (t + 1) * rows, col : col + span] = (
            jnp.concatenate(own, axis=0).T.astype(BF16)
        )


def kernel(
    mem_size,
    dp_size,
    cand_ids,
    cand_slot,
    out_bias,
    gain1,
    shift1,
    up_bias,
    down_bias,
    gain2,
    shift2,
    cache_hbm,
    img_hbm,
    w_key_hbm,
    w_value_hbm,
    w_query_hbm,
    w_out_hbm,
    w_up_hbm,
    w_down_hbm,
    arrived_out,
    cache,
    img,
    w_key,
    w_value,
    w_query,
    w_out,
    w_up,
    w_down,
    wide,
    requests,
    wanted,
    wanted_smem,
    outgoing,
    incoming,
    select,
    keys,
    values_t,
    context,
    finished,
    local_sem,
    smem_sem,
    ask_send,
    ask_recv,
    text_send,
    text_recv,
    out_send,
    out_recv,
    own_sem,
):
    dp = lax.axis_index("dp")
    mem = lax.axis_index("mem")
    words = cache.shape[1]
    piece_count = words // PIECE
    patches, images = img.shape[0:2]

    loads = [
        pltpu.make_async_copy(source, target, local_sem.at[index])
        for index, (source, target) in enumerate(
            [
                (cache_hbm, cache),
                (img_hbm, img),
                (w_key_hbm, w_key),
                (w_value_hbm, w_value),
                (w_query_hbm, w_query),
                (w_out_hbm, w_out),
                (w_up_hbm, w_up),
                (w_down_hbm, w_down),
            ]
        )
    ]
    for load in loads:
        load.start()

    barrier = pltpu.get_barrier_semaphore()

    def greet(step, carry):
        peer = lax.rem(mem + step, mem_size)
        pl.semaphore_signal(barrier, inc=1, device_id=(dp, peer), device_id_type=MESH)
        return carry

    lax.fori_loop(1, mem_size, greet, 0)
    for step in range(1, dp_size):
        pl.semaphore_signal(
            barrier, inc=1, device_id=(lax.rem(dp + step, dp_size), mem), device_id_type=MESH
        )
    plan(cand_ids, cand_slot, requests, select, cache.shape[0])
    pl.semaphore_wait(barrier, mem_size - 1 + dp_size - 1)

    def ask(step, carry):
        peer = lax.rem(mem + step, mem_size)
        pltpu.make_async_remote_copy(
            src_ref=requests.at[peer],
            dst_ref=wanted.at[mem],
            send_sem=ask_send,
            recv_sem=ask_recv,
            device_id=(dp, peer),
            device_id_type=MESH,
        ).start()
        return carry

    lax.fori_loop(1, mem_size, ask, 0)
    wanted[mem] = requests[mem]

    for load in loads[1:3]:
        load.wait()
    project_keys(img, w_key, keys, wide)

    others = pl.ds(0, mem_size - 1)
    pltpu.make_async_copy(wanted.at[others], wanted.at[others], ask_recv).wait()
    to_smem = pltpu.make_async_copy(wanted, wanted_smem, smem_sem)
    to_smem.start()
    loads[0].wait()
    to_smem.wait()

    def gather(peer, first):
        start = first * PIECE
        slots = [
            cache[wanted_smem[peer, 0, slot], start : start + PAIRED * PIECE, :].astype(F32)
            for slot in range(SLOTS)
        ]
        return [
            jnp.concatenate([rows[k * PIECE : (k + 1) * PIECE] for rows in slots], 0).astype(BF16)
            for k in range(PAIRED)
        ]

    def send(piece, peer):
        pltpu.make_async_remote_copy(
            src_ref=outgoing.at[piece, peer],
            dst_ref=incoming.at[piece, mem],
            send_sem=text_send.at[piece],
            recv_sem=text_recv.at[piece],
            device_id=(dp, peer),
            device_id_type=MESH,
        ).start()

    def partner(step):
        return lax.rem(mem + lax.rem(step * 13, mem_size), mem_size)

    for first in range(0, piece_count, PAIRED):
        for k, rows in enumerate(gather(mem, first)):
            incoming[first + k, mem] = rows

        def serve(step, carry, first=first):
            peer = partner(step)
            for k, rows in enumerate(gather(peer, first)):
                outgoing[first + k, peer] = rows
            send(first, peer)
            return carry

        def serve_next(step, carry, first=first):
            send(first + 1, partner(step))
            return carry

        lax.fori_loop(1, mem_size, serve, 0)
        lax.fori_loop(1, mem_size, serve_next, 0)

        if first == 0:
            loads[3].wait()
            project_values(img, w_value, values_t, wide)

    for load in loads[4:]:
        load.wait()

    group_rows = finished.shape[2]
    half_rows = group_rows // images

    def work(piece, carry):
        pltpu.make_async_copy(
            incoming.at[piece, others], incoming.at[piece, others], text_recv.at[piece]
        ).wait()
        arrived = incoming[piece].reshape(-1, incoming.shape[3])
        text = jnp.dot(select[...], arrived, preferred_element_type=F32)
        text_rows = text.astype(BF16)
        queries = jnp.dot(text_rows, w_query[...], preferred_element_type=F32).astype(BF16)
        attend(queries, keys, values_t, context, patches)
        attended = jnp.dot(context[...], w_out[...], preferred_element_type=F32)
        first_out = normalize(
            attended + spread_lanes(out_bias) + text_rows.astype(F32), spread_lanes(gain1), spread_lanes(shift1)
        ).astype(BF16)
        hidden = jnp.dot(first_out, w_up[...], preferred_element_type=F32) + spread_lanes(up_bias)
        hidden = (0.5 * hidden * (1.0 + lax.erf(hidden * 0.5**0.5))).astype(BF16)
        output = jnp.dot(hidden, w_down[...], preferred_element_type=F32)
        output = output + spread_lanes(down_bias) + first_out.astype(F32)
        encoded = normalize(output, spread_lanes(gain2), spread_lanes(shift2)).astype(BF16)
        for t in range(images):
            for group in range(dp_size):
                start = (t * dp_size + group) * half_rows
                finished[piece, group, t * half_rows : (t + 1) * half_rows, :] = encoded[
                    start : start + half_rows
                ]
        for step in range(1, dp_size):
            peer = lax.rem(dp + step, dp_size)
            pltpu.make_async_remote_copy(
                src_ref=finished.at[piece, peer],
                dst_ref=arrived_out.at[piece, dp],
                send_sem=out_send,
                recv_sem=out_recv,
                device_id=(peer, mem),
                device_id_type=MESH,
            ).start()
        pltpu.make_async_copy(
            finished.at[piece, dp], arrived_out.at[piece, dp], own_sem
        ).start()
        return carry

    lax.fori_loop(0, piece_count, work, 0)

    pltpu.make_async_copy(requests.at[others], requests.at[others], ask_send).wait()

    def drain(piece, carry):
        pltpu.make_async_copy(
            outgoing.at[piece, others], outgoing.at[piece, others], text_send.at[piece]
        ).wait()
        return carry

    lax.fori_loop(0, piece_count, drain, 0)
    sent = finished.at[:, pl.ds(0, dp_size - 1)]
    pltpu.make_async_copy(sent, sent, out_send).wait()
    came = arrived_out.at[:, pl.ds(0, dp_size - 1)]
    pltpu.make_async_copy(came, came, out_recv).wait()
    own = arrived_out.at[:, pl.ds(0, 1)]
    pltpu.make_async_copy(own, own, own_sem).wait()


def assemble(arrived, out):
    pieces = [arrived[piece, 0].astype(F32) for piece in range(arrived.shape[0])]
    for pair in range(out.shape[0]):
        rows = slice(pair * PIECE, (pair + 1) * PIECE)
        out[pair] = jnp.concatenate([piece[rows] for piece in pieces], axis=0).astype(BF16)


def on_device(
    images,
    text_cache,
    cand_ids,
    cand_slot,
    w_query,
    w_key,
    w_value,
    w_out,
    out_bias,
    norm1_gain,
    norm1_shift,
    w_up,
    up_bias,
    w_down,
    down_bias,
    norm2_gain,
    norm2_shift,
):
    mem_size = lax.axis_size("mem")
    dp_size = lax.axis_size("dp")
    img_local, cand_count = cand_ids.shape
    word_count, width = text_cache.shape[1:]
    patches = images.shape[1]
    hidden_width = w_up.shape[1]
    pair_count = img_local * cand_count
    piece_count = word_count // PIECE
    piece_rows = pair_count * PIECE
    slot_rows = SLOTS * PIECE
    padded = -(-patches // 16) * 16
    padded_lanes = -(-patches // LANES) * LANES

    vmem = pl.BlockSpec(memory_space=pltpu.VMEM)
    smem = pl.BlockSpec(memory_space=pltpu.SMEM)
    anywhere = pl.BlockSpec(memory_space=pl.ANY)
    group_rows = piece_rows // dp_size
    result = pl.pallas_call(
        functools.partial(kernel, mem_size, dp_size),
        out_shape=jax.ShapeDtypeStruct((piece_count, dp_size, group_rows, width), BF16),
        in_specs=[smem] * 2 + [vmem] * 7 + [anywhere] * 8,
        out_specs=anywhere,
        scratch_shapes=[
            pltpu.VMEM(text_cache.shape, BF16),
            pltpu.VMEM((patches, img_local, width), BF16),
            pltpu.VMEM((width, width), BF16),
            pltpu.VMEM((width, width), BF16),
            pltpu.VMEM((width, width), BF16),
            pltpu.VMEM((width, width), BF16),
            pltpu.VMEM((width, hidden_width), BF16),
            pltpu.VMEM((hidden_width, width), BF16),
            pltpu.VMEM((2, patches // 16 * 16 * img_local, LANES), F32),
            pltpu.VMEM((mem_size, 1, LANES), jnp.int32),
            pltpu.VMEM((mem_size, 1, LANES), jnp.int32),
            pltpu.SMEM((mem_size, 1, LANES), jnp.int32),
            pltpu.VMEM((piece_count, mem_size, slot_rows, width), BF16),
            pltpu.VMEM((piece_count, mem_size, slot_rows, width), BF16),
            pltpu.VMEM((piece_rows, mem_size * slot_rows), BF16),
            pltpu.VMEM((img_local, padded, width), BF16),
            pltpu.VMEM((img_local, width, padded_lanes), BF16),
            pltpu.VMEM((piece_rows, width), BF16),
            pltpu.VMEM((piece_count, dp_size, group_rows, width), BF16),
            pltpu.SemaphoreType.DMA((8,)),
            pltpu.SemaphoreType.DMA,
            pltpu.SemaphoreType.DMA,
            pltpu.SemaphoreType.DMA,
            pltpu.SemaphoreType.DMA((piece_count,)),
            pltpu.SemaphoreType.DMA((piece_count,)),
            pltpu.SemaphoreType.DMA,
            pltpu.SemaphoreType.DMA,
            pltpu.SemaphoreType.DMA,
        ],
        compiler_params=pltpu.CompilerParams(
            collective_id=0, has_side_effects=True, vmem_limit_bytes=60 * 2**20
        ),
    )(
        cand_ids,
        cand_slot,
        *(
            vector.reshape(-1, LANES)
            for vector in (
                out_bias,
                norm1_gain,
                norm1_shift,
                up_bias,
                down_bias,
                norm2_gain,
                norm2_shift,
            )
        ),
        text_cache,
        images.transpose(1, 0, 2),
        w_key,
        w_value,
        w_query,
        w_out,
        w_up,
        w_down,
    )
    pairs = pair_count // dp_size
    return pl.pallas_call(
        assemble,
        grid=(dp_size,),
        out_shape=jax.ShapeDtypeStruct((pair_count, word_count, width), BF16),
        in_specs=[pl.BlockSpec((piece_count, 1, group_rows, width), lambda s: (0, s, 0, 0))],
        out_specs=pl.BlockSpec((pairs, word_count, width), lambda s: (s, 0, 0)),
        compiler_params=pltpu.CompilerParams(vmem_limit_bytes=60 * 2**20),
    )(result)


def solution(mesh):
    split = P(("dp", "mem"), None, None)
    ids = P(("dp", "mem"), None)
    in_specs = (split, P("mem", None, None), ids, ids) + (P(),) * 13
    return jax.shard_map(
        on_device, mesh=mesh, in_specs=in_specs, out_specs=split, check_vma=False
    )
```

```python
import functools
import math

import jax
import jax.numpy as jnp
from jax import lax
from jax.experimental import pallas as pl
from jax.experimental.pallas import tpu as pltpu
from jax.sharding import PartitionSpec as P

MESH = pl.DeviceIdType.MESH
F32 = jnp.float32
BF16 = jnp.bfloat16
HEADS = 12
NORM_EPS = 1e-06
PIECE = 4
PAIRED = 2
SLOTS = 2
LANES = 128
NT = (((1,), (1,)), ((), ()))


def normalize(values, gain, shift):
    center = values - jnp.mean(values, axis=-1, keepdims=True)
    spread = jnp.mean(center * center, axis=-1, keepdims=True)
    return center * lax.rsqrt(spread + NORM_EPS) * gain + shift


def project_images(img, weight, wide, store):
    patches, images, width = img.shape
    whole = patches // 16 * 16
    rest = patches - whole
    body = img[0:whole].reshape(whole * images, width)
    tail = img[whole:patches].reshape(rest * images, width)
    tail_rows = jnp.concatenate(
        [tail.astype(F32), jnp.zeros((16 - rest * images, width), F32)], axis=0
    ).astype(BF16)
    for col in range(0, width, 2 * LANES):
        double = slice(col, col + 2 * LANES)
        product = jnp.dot(body, weight[:, double], preferred_element_type=F32)
        last = jnp.dot(tail_rows, weight[:, double], preferred_element_type=F32)
        for side in range(2):
            here = slice(side * LANES, (side + 1) * LANES)
            wide[side] = product[:, here]
            for t in range(images):
                rows = wide[side, pl.ds(t, whole, stride=images), :]
                ends = [last[t + images * p : t + images * p + 1, here] for p in range(rest)]
                store(t, col + side * LANES, rows, ends)


def project_keys(img, w_key, keys, wide):
    def store(t, col, rows, ends):
        cols = slice(col, col + LANES)
        whole, rest = rows.shape[0], len(ends)
        ends = [*ends, jnp.zeros((16 - rest, LANES), F32)]
        keys[t, 0:whole, cols] = rows.astype(BF16)
        keys[t, whole : whole + 16, cols] = jnp.concatenate(ends, axis=0).astype(BF16)

    project_images(img, w_key, wide, store)


def project_values(img, w_value, values_t, wide):
    def store(t, col, rows, ends):
        pad = jnp.zeros((values_t.shape[2] - rows.shape[0] - len(ends), LANES), F32)
        rows = jnp.concatenate([rows, *ends, pad], axis=0)
        values_t[t, col : col + LANES, :] = rows.T.astype(BF16)

    project_images(img, w_value, wide, store)


def spread_lanes(ref):
    return jnp.concatenate([ref[row : row + 1, :] for row in range(ref.shape[0])], axis=1)


def plan(cand_ids, cand_slot, requests, select, cap_local):
    mem_size = requests.shape[0]
    images, cands = cand_ids.shape
    pairs = [(t, j) for t in range(images) for j in range(cands)]
    owners = [lax.div(cand_ids[t, j], cap_local) for t, j in pairs]
    rows = [lax.rem(cand_ids[t, j], cap_local) for t, j in pairs]
    shape = (max(mem_size, len(pairs)), LANES)
    sub = lax.broadcasted_iota(jnp.int32, shape, 0)
    lane = lax.broadcasted_iota(jnp.int32, shape, 1)
    slot_key = jnp.where(lane < SLOTS, sub * SLOTS + lane, -1)
    table = jnp.zeros(shape, jnp.int32)
    slot_of = jnp.zeros(shape, jnp.int32)
    for n, (t, j) in enumerate(pairs):
        slot = owners[n] * SLOTS
        for before in range(n):
            slot = slot + jnp.where(owners[before] == owners[n], 1, 0)
        table = jnp.where(slot_key == slot, rows[n], table)
        slot_of = jnp.where(sub == t * cands + cand_slot[t, j], slot, slot_of)
    for shard in range(mem_size):
        requests[shard] = table[shard : shard + 1, :]
    word = lax.broadcasted_iota(jnp.int32, (PIECE, LANES), 0)
    wanted_rows = jnp.concatenate(
        [
            jnp.broadcast_to(slot_of[n : n + 1, :], (PIECE, LANES)) * PIECE + word
            for n in range(len(pairs))
        ],
        axis=0,
    )
    for col in range(0, select.shape[1], LANES):
        here = lax.broadcasted_iota(jnp.int32, wanted_rows.shape, 1) + col
        select[:, col : col + LANES] = jnp.where(wanted_rows == here, 1.0, 0.0).astype(BF16)


def head_scores(queries, keys, t, col, rows, span, head_dim):
    these = queries[t * rows : (t + 1) * rows, col : col + span].astype(F32)
    head = lax.broadcasted_iota(jnp.int32, these.shape, 1) // head_dim
    stacked = jnp.concatenate(
        [jnp.where(head == h, these, 0.0) for h in range(span // head_dim)], axis=0
    )
    return lax.dot_general(
        keys[t, :, col : col + span], stacked.astype(BF16), NT, preferred_element_type=F32
    )


def exponentials(scores, patches, scale):
    whole = patches // 16 * 16
    tail = scores[whole:]
    row = lax.broadcasted_iota(jnp.int32, tail.shape, 0)
    tail = jnp.where(row < patches - whole, tail, -1e30)
    top = jnp.maximum(
        jnp.max(scores[0:whole], axis=0, keepdims=True), jnp.max(tail, axis=0, keepdims=True)
    )
    factor = scale * math.log2(math.e)
    parts, total = [], 0.0
    for start in range(0, whole + 16, 16):
        part = tail if start == whole else scores[start : start + 16]
        part = jnp.exp2((part - top) * factor)
        parts.append(part.astype(BF16))
        total = total + part
    return jnp.concatenate(parts, axis=0), jnp.sum(total, axis=0, keepdims=True)


def attend(queries, keys, values_t, context, patches):
    images, padded, width = keys.shape
    rows = queries.shape[0] // images
    head_dim = width // HEADS
    span = 2 * LANES // rows * head_dim
    scale = head_dim ** (-0.5)
    order = [(t, col) for t in range(images) for col in range(0, width, span)]
    scores = [head_scores(queries, keys, t, col, rows, span, head_dim) for t, col in order]
    probs = [exponentials(one, patches, scale) for one in scores]
    for (t, col), (one, total) in zip(order, probs):
        mixed = jnp.dot(values_t[t, col : col + span, 0:padded], one, preferred_element_type=F32)
        mixed = mixed * (1.0 / total)
        own = [
            mixed[h * head_dim : (h + 1) * head_dim, h * rows : (h + 1) * rows]
            for h in range(span // head_dim)
        ]
        context[t * rows : (t + 1) * rows, col : col + span] = (
            jnp.concatenate(own, axis=0).T.astype(BF16)
        )


def kernel(
    mem_size,
    dp_size,
    cand_ids,
    cand_slot,
    out_bias,
    gain1,
    shift1,
    up_bias,
    down_bias,
    gain2,
    shift2,
    cache_hbm,
    img_hbm,
    w_key_hbm,
    w_value_hbm,
    w_query_hbm,
    w_out_hbm,
    w_up_hbm,
    w_down_hbm,
    arrived_out,
    cache,
    img,
    w_key,
    w_value,
    w_query,
    w_out,
    w_up,
    w_down,
    wide,
    requests,
    wanted,
    wanted_smem,
    outgoing,
    incoming,
    select,
    keys,
    values_t,
    context,
    unfinished,
    finished,
    local_sem,
    smem_sem,
    ask_send,
    ask_recv,
    text_send,
    text_recv,
    out_send,
    out_recv,
    own_sem,
):
    dp = lax.axis_index("dp")
    mem = lax.axis_index("mem")
    words = cache.shape[1]
    piece_count = words // PIECE
    patches, images = img.shape[0:2]

    barrier = pltpu.get_barrier_semaphore()

    def greet(step, carry):
        peer = lax.rem(mem + step, mem_size)
        pl.semaphore_signal(barrier, inc=1, device_id=(dp, peer), device_id_type=MESH)
        return carry

    lax.fori_loop(1, mem_size, greet, 0)
    for step in range(1, dp_size):
        pl.semaphore_signal(
            barrier, inc=1, device_id=(lax.rem(dp + step, dp_size), mem), device_id_type=MESH
        )
    loads = [
        pltpu.make_async_copy(source, target, local_sem.at[index])
        for index, (source, target) in enumerate(
            [
                (cache_hbm, cache),
                (img_hbm, img),
                (w_key_hbm, w_key),
                (w_value_hbm, w_value),
                (w_query_hbm, w_query),
                (w_out_hbm, w_out),
                (w_up_hbm, w_up),
                (w_down_hbm, w_down),
            ]
        )
    ]
    for load in loads:
        load.start()

    plan(cand_ids, cand_slot, requests, select, cache.shape[0])
    pl.semaphore_wait(barrier, mem_size - 1 + dp_size - 1)

    def ask(step, carry):
        peer = lax.rem(mem + step, mem_size)
        pltpu.make_async_remote_copy(
            src_ref=requests.at[peer],
            dst_ref=wanted.at[mem],
            send_sem=ask_send,
            recv_sem=ask_recv,
            device_id=(dp, peer),
            device_id_type=MESH,
        ).start()
        return carry

    lax.fori_loop(1, mem_size, ask, 0)
    wanted[mem] = requests[mem]

    for load in loads[1:3]:
        load.wait()
    project_keys(img, w_key, keys, wide)

    others = pl.ds(0, mem_size - 1)
    pltpu.make_async_copy(wanted.at[others], wanted.at[others], ask_recv).wait()
    to_smem = pltpu.make_async_copy(wanted, wanted_smem, smem_sem)
    to_smem.start()
    loads[0].wait()
    to_smem.wait()

    def gather(peer, first):
        start = first * PIECE
        slots = [
            cache[wanted_smem[peer, 0, slot], start : start + PAIRED * PIECE, :].astype(F32)
            for slot in range(SLOTS)
        ]
        return [
            jnp.concatenate([rows[k * PIECE : (k + 1) * PIECE] for rows in slots], 0).astype(BF16)
            for k in range(PAIRED)
        ]

    def send(piece, peer):
        pltpu.make_async_remote_copy(
            src_ref=outgoing.at[piece, peer],
            dst_ref=incoming.at[piece, mem],
            send_sem=text_send.at[piece],
            recv_sem=text_recv.at[piece],
            device_id=(dp, peer),
            device_id_type=MESH,
        ).start()

    def partner(step):
        return lax.rem(mem + lax.rem(step * 13, mem_size), mem_size)

    for first in range(0, piece_count, PAIRED):
        for k, rows in enumerate(gather(mem, first)):
            incoming[first + k, mem] = rows

        def serve(step, carry, first=first):
            peer = partner(step)
            for k, rows in enumerate(gather(peer, first)):
                outgoing[first + k, peer] = rows
            send(first, peer)
            return carry

        def serve_next(step, carry, first=first):
            send(first + 1, partner(step))
            return carry

        lax.fori_loop(1, mem_size, serve, 0)
        lax.fori_loop(1, mem_size, serve_next, 0)

        if first == 0:
            loads[3].wait()
            project_values(img, w_value, values_t, wide)

    for load in loads[4:]:
        load.wait()

    group_rows = finished.shape[2]
    half_rows = group_rows // images

    def finish(piece):
        encoded = normalize(
            unfinished[...], spread_lanes(gain2), spread_lanes(shift2)
        ).astype(BF16)
        for t in range(images):
            for group in range(dp_size):
                start = (t * dp_size + group) * half_rows
                finished[piece, group, t * half_rows : (t + 1) * half_rows, :] = encoded[
                    start : start + half_rows
                ]

    def send_finished(piece):
        for step in sorted(range(1, dp_size), key=lambda hops: -min(hops, dp_size - hops)):
            peer = lax.rem(dp + step, dp_size)
            pltpu.make_async_remote_copy(
                src_ref=finished.at[piece, peer],
                dst_ref=arrived_out.at[piece, dp],
                send_sem=out_send,
                recv_sem=out_recv,
                device_id=(peer, mem),
                device_id_type=MESH,
            ).start()
        pltpu.make_async_copy(
            finished.at[piece, dp], arrived_out.at[piece, dp], own_sem
        ).start()

    def work(piece, carry):
        pltpu.make_async_copy(
            incoming.at[piece, others], incoming.at[piece, others], text_recv.at[piece]
        ).wait()
        before = lax.max(piece - 1, 0)
        finish(before)
        arrived = incoming[piece].reshape(-1, incoming.shape[3])
        text = jnp.dot(select[...], arrived, preferred_element_type=F32)
        text_rows = text.astype(BF16)
        queries = jnp.dot(text_rows, w_query[...], preferred_element_type=F32).astype(BF16)

        @pl.when(piece > 0)
        def _():
            send_finished(before)

        attend(queries, keys, values_t, context, patches)
        attended = jnp.dot(context[...], w_out[...], preferred_element_type=F32)
        first_out = normalize(
            attended + spread_lanes(out_bias) + text_rows.astype(F32),
            spread_lanes(gain1),
            spread_lanes(shift1),
        ).astype(BF16)
        hidden = jnp.dot(first_out, w_up[...], preferred_element_type=F32) + spread_lanes(up_bias)
        hidden = (0.5 * hidden * (1.0 + lax.erf(hidden * 0.5**0.5))).astype(BF16)
        output = jnp.dot(hidden, w_down[...], preferred_element_type=F32)
        unfinished[...] = output + spread_lanes(down_bias) + first_out.astype(F32)
        return carry

    unfinished[...] = jnp.zeros_like(unfinished)
    lax.fori_loop(0, piece_count, work, 0)
    finish(piece_count - 1)
    send_finished(piece_count - 1)

    pltpu.make_async_copy(requests.at[others], requests.at[others], ask_send).wait()

    def drain(piece, carry):
        pltpu.make_async_copy(
            outgoing.at[piece, others], outgoing.at[piece, others], text_send.at[piece]
        ).wait()
        return carry

    lax.fori_loop(0, piece_count, drain, 0)
    sent = finished.at[:, pl.ds(0, dp_size - 1)]
    pltpu.make_async_copy(sent, sent, out_send).wait()
    came = arrived_out.at[:, pl.ds(0, dp_size - 1)]
    pltpu.make_async_copy(came, came, out_recv).wait()
    own = arrived_out.at[:, pl.ds(0, 1)]
    pltpu.make_async_copy(own, own, own_sem).wait()


def assemble(arrived_hbm, out_hbm, arrived, out, in_sem, out_sem):
    sources, pieces, rows = arrived.shape[0:3]
    pairs = rows // PIECE
    loads = [
        pltpu.make_async_copy(arrived_hbm.at[:, source], arrived.at[source], in_sem.at[source])
        for source in range(sources)
    ]
    stores = [
        pltpu.make_async_copy(
            out.at[pl.ds(source * pairs, pairs)],
            out_hbm.at[pl.ds(source * pairs, pairs)],
            out_sem.at[source],
        )
        for source in range(sources)
    ]
    for load in loads:
        load.start()
    for source in range(sources):
        loads[source].wait()
        parts = [arrived[source, piece].astype(F32) for piece in range(pieces)]
        for pair in range(pairs):
            words = [part[pair * PIECE : (pair + 1) * PIECE] for part in parts]
            out[source * pairs + pair] = jnp.concatenate(words, axis=0).astype(BF16)
        stores[source].start()
    for store in stores:
        store.wait()


def on_device(
    images,
    text_cache,
    cand_ids,
    cand_slot,
    w_query,
    w_key,
    w_value,
    w_out,
    out_bias,
    norm1_gain,
    norm1_shift,
    w_up,
    up_bias,
    w_down,
    down_bias,
    norm2_gain,
    norm2_shift,
):
    mem_size = lax.axis_size("mem")
    dp_size = lax.axis_size("dp")
    img_local, cand_count = cand_ids.shape
    word_count, width = text_cache.shape[1:]
    patches = images.shape[1]
    hidden_width = w_up.shape[1]
    pair_count = img_local * cand_count
    piece_count = word_count // PIECE
    piece_rows = pair_count * PIECE
    slot_rows = SLOTS * PIECE
    padded = -(-patches // 16) * 16
    padded_lanes = -(-patches // LANES) * LANES

    vmem = pl.BlockSpec(memory_space=pltpu.VMEM)
    smem = pl.BlockSpec(memory_space=pltpu.SMEM)
    anywhere = pl.BlockSpec(memory_space=pl.ANY)
    group_rows = piece_rows // dp_size
    result = pl.pallas_call(
        functools.partial(kernel, mem_size, dp_size),
        out_shape=jax.ShapeDtypeStruct((piece_count, dp_size, group_rows, width), BF16),
        in_specs=[smem] * 2 + [vmem] * 7 + [anywhere] * 8,
        out_specs=anywhere,
        scratch_shapes=[
            pltpu.VMEM(text_cache.shape, BF16),
            pltpu.VMEM((patches, img_local, width), BF16),
            pltpu.VMEM((width, width), BF16),
            pltpu.VMEM((width, width), BF16),
            pltpu.VMEM((width, width), BF16),
            pltpu.VMEM((width, width), BF16),
            pltpu.VMEM((width, hidden_width), BF16),
            pltpu.VMEM((hidden_width, width), BF16),
            pltpu.VMEM((2, patches // 16 * 16 * img_local, LANES), F32),
            pltpu.VMEM((mem_size, 1, LANES), jnp.int32),
            pltpu.VMEM((mem_size, 1, LANES), jnp.int32),
            pltpu.SMEM((mem_size, 1, LANES), jnp.int32),
            pltpu.VMEM((piece_count, mem_size, slot_rows, width), BF16),
            pltpu.VMEM((piece_count, mem_size, slot_rows, width), BF16),
            pltpu.VMEM((piece_rows, mem_size * slot_rows), BF16),
            pltpu.VMEM((img_local, padded, width), BF16),
            pltpu.VMEM((img_local, width, padded_lanes), BF16),
            pltpu.VMEM((piece_rows, width), BF16),
            pltpu.VMEM((piece_rows, width), F32),
            pltpu.VMEM((piece_count, dp_size, group_rows, width), BF16),
            pltpu.SemaphoreType.DMA((8,)),
            pltpu.SemaphoreType.DMA,
            pltpu.SemaphoreType.DMA,
            pltpu.SemaphoreType.DMA,
            pltpu.SemaphoreType.DMA((piece_count,)),
            pltpu.SemaphoreType.DMA((piece_count,)),
            pltpu.SemaphoreType.DMA,
            pltpu.SemaphoreType.DMA,
            pltpu.SemaphoreType.DMA,
        ],
        compiler_params=pltpu.CompilerParams(
            collective_id=0, has_side_effects=True, vmem_limit_bytes=60 * 2**20
        ),
    )(
        cand_ids,
        cand_slot,
        *(
            vector.reshape(-1, LANES)
            for vector in (
                out_bias,
                norm1_gain,
                norm1_shift,
                up_bias,
                down_bias,
                norm2_gain,
                norm2_shift,
            )
        ),
        text_cache,
        images.transpose(1, 0, 2),
        w_key,
        w_value,
        w_query,
        w_out,
        w_up,
        w_down,
    )
    return pl.pallas_call(
        assemble,
        out_shape=jax.ShapeDtypeStruct((pair_count, word_count, width), BF16),
        in_specs=[anywhere],
        out_specs=anywhere,
        scratch_shapes=[
            pltpu.VMEM((dp_size, piece_count, group_rows, width), BF16),
            pltpu.VMEM((pair_count, word_count, width), BF16),
            pltpu.SemaphoreType.DMA((dp_size,)),
            pltpu.SemaphoreType.DMA((dp_size,)),
        ],
        compiler_params=pltpu.CompilerParams(vmem_limit_bytes=60 * 2**20),
    )(result)


def solution(mesh):
    split = P(("dp", "mem"), None, None)
    ids = P(("dp", "mem"), None)
    in_specs = (split, P("mem", None, None), ids, ids) + (P(),) * 13
    return jax.shard_map(
        on_device, mesh=mesh, in_specs=in_specs, out_specs=split, check_vma=False
    )
```

```python
import functools
import math

import jax
import jax.numpy as jnp
from jax import lax
from jax.experimental import pallas as pl
from jax.experimental.pallas import tpu as pltpu
from jax.sharding import PartitionSpec as P

MESH = pl.DeviceIdType.MESH
F32 = jnp.float32
BF16 = jnp.bfloat16
HEADS = 12
NORM_EPS = 1e-06
PIECE = 4
PAIRED = 2
SLOTS = 2
LANES = 128
NT = (((1,), (1,)), ((), ()))


def normalize(values, gain, shift):
    center = values - jnp.mean(values, axis=-1, keepdims=True)
    spread = jnp.mean(center * center, axis=-1, keepdims=True)
    return center * lax.rsqrt(spread + NORM_EPS) * gain + shift


def project_images(img, weight, wide, store):
    patches, images, width = img.shape
    whole = patches // 16 * 16
    rest = patches - whole
    body = img[0:whole].reshape(whole * images, width)
    tail = img[whole:patches].reshape(rest * images, width)
    tail_rows = jnp.concatenate(
        [tail.astype(F32), jnp.zeros((16 - rest * images, width), F32)], axis=0
    ).astype(BF16)
    for col in range(0, width, 2 * LANES):
        double = slice(col, col + 2 * LANES)
        product = jnp.dot(body, weight[:, double], preferred_element_type=F32)
        last = jnp.dot(tail_rows, weight[:, double], preferred_element_type=F32)
        for side in range(2):
            here = slice(side * LANES, (side + 1) * LANES)
            wide[side] = product[:, here]
            for t in range(images):
                rows = wide[side, pl.ds(t, whole, stride=images), :]
                ends = [last[t + images * p : t + images * p + 1, here] for p in range(rest)]
                store(t, col + side * LANES, rows, ends)


def project_keys(img, w_key, keys, wide):
    def store(t, col, rows, ends):
        cols = slice(col, col + LANES)
        whole, rest = rows.shape[0], len(ends)
        ends = [*ends, jnp.zeros((16 - rest, LANES), F32)]
        keys[t, 0:whole, cols] = rows.astype(BF16)
        keys[t, whole : whole + 16, cols] = jnp.concatenate(ends, axis=0).astype(BF16)

    project_images(img, w_key, wide, store)


def project_values(img, w_value, values_t, wide):
    def store(t, col, rows, ends):
        pad = jnp.zeros((values_t.shape[2] - rows.shape[0] - len(ends), LANES), F32)
        rows = jnp.concatenate([rows, *ends, pad], axis=0)
        values_t[t, col : col + LANES, :] = rows.T.astype(BF16)

    project_images(img, w_value, wide, store)


def spread_lanes(ref):
    return jnp.concatenate([ref[row : row + 1, :] for row in range(ref.shape[0])], axis=1)


def plan(cand_ids, cand_slot, requests, select, cap_local):
    mem_size = requests.shape[0]
    images, cands = cand_ids.shape
    pairs = [(t, j) for t in range(images) for j in range(cands)]
    owners = [lax.div(cand_ids[t, j], cap_local) for t, j in pairs]
    rows = [lax.rem(cand_ids[t, j], cap_local) for t, j in pairs]
    shape = (max(mem_size, len(pairs)), LANES)
    sub = lax.broadcasted_iota(jnp.int32, shape, 0)
    lane = lax.broadcasted_iota(jnp.int32, shape, 1)
    slot_key = jnp.where(lane < SLOTS, sub * SLOTS + lane, -1)
    table = jnp.zeros(shape, jnp.int32)
    slot_of = jnp.zeros(shape, jnp.int32)
    for n, (t, j) in enumerate(pairs):
        slot = owners[n] * SLOTS
        for before in range(n):
            slot = slot + jnp.where(owners[before] == owners[n], 1, 0)
        table = jnp.where(slot_key == slot, rows[n], table)
        slot_of = jnp.where(sub == t * cands + cand_slot[t, j], slot, slot_of)
    for shard in range(mem_size):
        requests[shard] = table[shard : shard + 1, :]
    word = lax.broadcasted_iota(jnp.int32, (PIECE, LANES), 0)
    wanted_rows = jnp.concatenate(
        [
            jnp.broadcast_to(slot_of[n : n + 1, :], (PIECE, LANES)) * PIECE + word
            for n in range(len(pairs))
        ],
        axis=0,
    )
    for col in range(0, select.shape[1], LANES):
        here = lax.broadcasted_iota(jnp.int32, wanted_rows.shape, 1) + col
        select[:, col : col + LANES] = jnp.where(wanted_rows == here, 1.0, 0.0).astype(BF16)


def head_scores(queries, keys, t, col, rows, span, head_dim):
    these = queries[t * rows : (t + 1) * rows, col : col + span].astype(F32)
    head = lax.broadcasted_iota(jnp.int32, these.shape, 1) // head_dim
    stacked = jnp.concatenate(
        [jnp.where(head == h, these, 0.0) for h in range(span // head_dim)], axis=0
    )
    return lax.dot_general(
        keys[t, :, col : col + span], stacked.astype(BF16), NT, preferred_element_type=F32
    )


def exponentials(scores, patches, scale):
    whole = patches // 16 * 16
    tail = scores[whole:]
    row = lax.broadcasted_iota(jnp.int32, tail.shape, 0)
    tail = jnp.where(row < patches - whole, tail, -1e30)
    top = jnp.maximum(
        jnp.max(scores[0:whole], axis=0, keepdims=True), jnp.max(tail, axis=0, keepdims=True)
    )
    factor = scale * math.log2(math.e)
    parts, total = [], 0.0
    for start in range(0, whole + 16, 16):
        part = tail if start == whole else scores[start : start + 16]
        part = jnp.exp2((part - top) * factor)
        parts.append(part.astype(BF16))
        total = total + part
    return jnp.concatenate(parts, axis=0), jnp.sum(total, axis=0, keepdims=True)


def attend(queries, keys, values_t, context, patches):
    images, padded, width = keys.shape
    rows = queries.shape[0] // images
    head_dim = width // HEADS
    span = 2 * LANES // rows * head_dim
    scale = head_dim ** (-0.5)
    order = [(t, col) for t in range(images) for col in range(0, width, span)]
    scores = [head_scores(queries, keys, t, col, rows, span, head_dim) for t, col in order]
    probs = [exponentials(one, patches, scale) for one in scores]
    for (t, col), (one, total) in zip(order, probs):
        mixed = jnp.dot(values_t[t, col : col + span, 0:padded], one, preferred_element_type=F32)
        mixed = mixed * (1.0 / total)
        own = [
            mixed[h * head_dim : (h + 1) * head_dim, h * rows : (h + 1) * rows]
            for h in range(span // head_dim)
        ]
        context[t * rows : (t + 1) * rows, col : col + span] = (
            jnp.concatenate(own, axis=0).T.astype(BF16)
        )


def kernel(
    mem_size,
    dp_size,
    cand_ids,
    cand_slot,
    out_bias,
    gain1,
    shift1,
    up_bias,
    down_bias,
    gain2,
    shift2,
    cache_hbm,
    img_hbm,
    w_key_hbm,
    w_value_hbm,
    w_query_hbm,
    w_out_hbm,
    w_up_hbm,
    w_down_hbm,
    arrived_out,
    cache,
    img,
    w_key,
    w_value,
    w_query,
    w_out,
    w_up,
    w_down,
    wide,
    requests,
    wanted,
    wanted_smem,
    outgoing,
    incoming,
    select,
    keys,
    values_t,
    context,
    unfinished,
    finished,
    local_sem,
    smem_sem,
    ask_send,
    ask_recv,
    text_send,
    text_recv,
    out_send,
    out_recv,
    own_sem,
):
    dp = lax.axis_index("dp")
    mem = lax.axis_index("mem")
    words = cache.shape[1]
    piece_count = words // PIECE
    patches, images = img.shape[0:2]

    barrier = pltpu.get_barrier_semaphore()

    def far_first(step):
        return lax.rem(step + mem_size // 2 - 2, mem_size - 1) + 1

    def greet(step, carry):
        peer = lax.rem(mem + far_first(step), mem_size)
        pl.semaphore_signal(barrier, inc=1, device_id=(dp, peer), device_id_type=MESH)
        return carry

    lax.fori_loop(1, mem_size, greet, 0)
    for step in range(1, dp_size):
        pl.semaphore_signal(
            barrier, inc=1, device_id=(lax.rem(dp + step, dp_size), mem), device_id_type=MESH
        )
    loads = [
        pltpu.make_async_copy(source, target, local_sem.at[index])
        for index, (source, target) in enumerate(
            [
                (cache_hbm, cache),
                (img_hbm, img),
                (w_key_hbm, w_key),
                (w_value_hbm, w_value),
                (w_query_hbm, w_query),
                (w_out_hbm, w_out),
                (w_up_hbm, w_up),
                (w_down_hbm, w_down),
            ]
        )
    ]
    for load in loads:
        load.start()

    plan(cand_ids, cand_slot, requests, select, cache.shape[0])
    pl.semaphore_wait(barrier, mem_size - 1 + dp_size - 1)

    def ask(step, carry):
        peer = lax.rem(mem + far_first(step), mem_size)
        pltpu.make_async_remote_copy(
            src_ref=requests.at[peer],
            dst_ref=wanted.at[mem],
            send_sem=ask_send,
            recv_sem=ask_recv,
            device_id=(dp, peer),
            device_id_type=MESH,
        ).start()
        return carry

    lax.fori_loop(1, mem_size, ask, 0)
    wanted[mem] = requests[mem]

    for load in loads[1:3]:
        load.wait()
    project_keys(img, w_key, keys, wide)

    others = pl.ds(0, mem_size - 1)
    pltpu.make_async_copy(wanted.at[others], wanted.at[others], ask_recv).wait()
    to_smem = pltpu.make_async_copy(wanted, wanted_smem, smem_sem)
    to_smem.start()
    loads[0].wait()
    to_smem.wait()

    def gather(peer, first):
        start = first * PIECE
        slots = [
            cache[wanted_smem[peer, 0, slot], start : start + PAIRED * PIECE, :].astype(F32)
            for slot in range(SLOTS)
        ]
        return [
            jnp.concatenate([rows[k * PIECE : (k + 1) * PIECE] for rows in slots], 0).astype(BF16)
            for k in range(PAIRED)
        ]

    def send(piece, peer):
        pltpu.make_async_remote_copy(
            src_ref=outgoing.at[piece, peer],
            dst_ref=incoming.at[piece, mem],
            send_sem=text_send.at[piece],
            recv_sem=text_recv.at[piece],
            device_id=(dp, peer),
            device_id_type=MESH,
        ).start()

    def partner(step):
        return lax.rem(mem + lax.rem(step * 13, mem_size), mem_size)

    for first in range(0, piece_count, PAIRED):
        for k, rows in enumerate(gather(mem, first)):
            incoming[first + k, mem] = rows

        def serve(step, carry, first=first):
            peer = partner(step)
            for k, rows in enumerate(gather(peer, first)):
                outgoing[first + k, peer] = rows
            send(first, peer)
            return carry

        def serve_next(step, carry, first=first):
            send(first + 1, partner(step))
            return carry

        lax.fori_loop(1, mem_size, serve, 0)
        lax.fori_loop(1, mem_size, serve_next, 0)

        if first == 0:
            loads[3].wait()
            project_values(img, w_value, values_t, wide)

    for load in loads[4:]:
        load.wait()

    group_rows = finished.shape[2]
    half_rows = group_rows // images

    def finish(piece):
        encoded = normalize(
            unfinished[...], spread_lanes(gain2), spread_lanes(shift2)
        ).astype(BF16)
        for t in range(images):
            for group in range(dp_size):
                start = (t * dp_size + group) * half_rows
                finished[piece, group, t * half_rows : (t + 1) * half_rows, :] = encoded[
                    start : start + half_rows
                ]

    def send_finished(piece):
        for step in sorted(range(1, dp_size), key=lambda hops: -min(hops, dp_size - hops)):
            peer = lax.rem(dp + step, dp_size)
            pltpu.make_async_remote_copy(
                src_ref=finished.at[piece, peer],
                dst_ref=arrived_out.at[piece, dp],
                send_sem=out_send,
                recv_sem=out_recv,
                device_id=(peer, mem),
                device_id_type=MESH,
            ).start()
        pltpu.make_async_copy(
            finished.at[piece, dp], arrived_out.at[piece, dp], own_sem
        ).start()

    def work(piece, carry):
        pltpu.make_async_copy(
            incoming.at[piece, others], incoming.at[piece, others], text_recv.at[piece]
        ).wait()
        before = lax.max(piece - 1, 0)
        finish(before)
        arrived = incoming[piece].reshape(-1, incoming.shape[3])
        text = jnp.dot(select[...], arrived, preferred_element_type=F32)
        text_rows = text.astype(BF16)
        queries = jnp.dot(text_rows, w_query[...], preferred_element_type=F32).astype(BF16)

        @pl.when(piece > 0)
        def _():
            send_finished(before)

        attend(queries, keys, values_t, context, patches)
        attended = jnp.dot(context[...], w_out[...], preferred_element_type=F32)
        first_out = normalize(
            attended + spread_lanes(out_bias) + text_rows.astype(F32),
            spread_lanes(gain1),
            spread_lanes(shift1),
        ).astype(BF16)
        hidden = jnp.dot(first_out, w_up[...], preferred_element_type=F32) + spread_lanes(up_bias)
        hidden = (0.5 * hidden * (1.0 + lax.erf(hidden * 0.5**0.5))).astype(BF16)
        output = jnp.dot(hidden, w_down[...], preferred_element_type=F32)
        unfinished[...] = output + spread_lanes(down_bias) + first_out.astype(F32)
        return carry

    unfinished[...] = jnp.zeros_like(unfinished)
    lax.fori_loop(0, piece_count, work, 0)
    finish(piece_count - 1)
    send_finished(piece_count - 1)

    pltpu.make_async_copy(requests.at[others], requests.at[others], ask_send).wait()

    def drain(piece, carry):
        pltpu.make_async_copy(
            outgoing.at[piece, others], outgoing.at[piece, others], text_send.at[piece]
        ).wait()
        return carry

    lax.fori_loop(0, piece_count, drain, 0)
    sent = finished.at[:, pl.ds(0, dp_size - 1)]
    pltpu.make_async_copy(sent, sent, out_send).wait()
    came = arrived_out.at[:, pl.ds(0, dp_size - 1)]
    pltpu.make_async_copy(came, came, out_recv).wait()
    own = arrived_out.at[:, pl.ds(0, 1)]
    pltpu.make_async_copy(own, own, own_sem).wait()


def assemble(arrived_hbm, out_hbm, arrived, out, in_sem, out_sem):
    sources, pieces, rows = arrived.shape[0:3]
    pairs = rows // PIECE
    loads = [
        pltpu.make_async_copy(arrived_hbm.at[:, source], arrived.at[source], in_sem.at[source])
        for source in range(sources)
    ]
    stores = [
        pltpu.make_async_copy(
            out.at[pl.ds(source * pairs, pairs)],
            out_hbm.at[pl.ds(source * pairs, pairs)],
            out_sem.at[source],
        )
        for source in range(sources)
    ]
    for load in loads:
        load.start()
    for source in range(sources):
        loads[source].wait()
        parts = [arrived[source, piece].astype(F32) for piece in range(pieces)]
        for pair in range(pairs):
            words = [part[pair * PIECE : (pair + 1) * PIECE] for part in parts]
            out[source * pairs + pair] = jnp.concatenate(words, axis=0).astype(BF16)
        stores[source].start()
    for store in stores:
        store.wait()


def on_device(
    images,
    text_cache,
    cand_ids,
    cand_slot,
    w_query,
    w_key,
    w_value,
    w_out,
    out_bias,
    norm1_gain,
    norm1_shift,
    w_up,
    up_bias,
    w_down,
    down_bias,
    norm2_gain,
    norm2_shift,
):
    mem_size = lax.axis_size("mem")
    dp_size = lax.axis_size("dp")
    img_local, cand_count = cand_ids.shape
    word_count, width = text_cache.shape[1:]
    patches = images.shape[1]
    hidden_width = w_up.shape[1]
    pair_count = img_local * cand_count
    piece_count = word_count // PIECE
    piece_rows = pair_count * PIECE
    slot_rows = SLOTS * PIECE
    padded = -(-patches // 16) * 16
    padded_lanes = -(-patches // LANES) * LANES

    vmem = pl.BlockSpec(memory_space=pltpu.VMEM)
    smem = pl.BlockSpec(memory_space=pltpu.SMEM)
    anywhere = pl.BlockSpec(memory_space=pl.ANY)
    group_rows = piece_rows // dp_size
    result = pl.pallas_call(
        functools.partial(kernel, mem_size, dp_size),
        out_shape=jax.ShapeDtypeStruct((piece_count, dp_size, group_rows, width), BF16),
        in_specs=[smem] * 2 + [vmem] * 7 + [anywhere] * 8,
        out_specs=anywhere,
        scratch_shapes=[
            pltpu.VMEM(text_cache.shape, BF16),
            pltpu.VMEM((patches, img_local, width), BF16),
            pltpu.VMEM((width, width), BF16),
            pltpu.VMEM((width, width), BF16),
            pltpu.VMEM((width, width), BF16),
            pltpu.VMEM((width, width), BF16),
            pltpu.VMEM((width, hidden_width), BF16),
            pltpu.VMEM((hidden_width, width), BF16),
            pltpu.VMEM((2, patches // 16 * 16 * img_local, LANES), F32),
            pltpu.VMEM((mem_size, 1, LANES), jnp.int32),
            pltpu.VMEM((mem_size, 1, LANES), jnp.int32),
            pltpu.SMEM((mem_size, 1, LANES), jnp.int32),
            pltpu.VMEM((piece_count, mem_size, slot_rows, width), BF16),
            pltpu.VMEM((piece_count, mem_size, slot_rows, width), BF16),
            pltpu.VMEM((piece_rows, mem_size * slot_rows), BF16),
            pltpu.VMEM((img_local, padded, width), BF16),
            pltpu.VMEM((img_local, width, padded_lanes), BF16),
            pltpu.VMEM((piece_rows, width), BF16),
            pltpu.VMEM((piece_rows, width), F32),
            pltpu.VMEM((piece_count, dp_size, group_rows, width), BF16),
            pltpu.SemaphoreType.DMA((8,)),
            pltpu.SemaphoreType.DMA,
            pltpu.SemaphoreType.DMA,
            pltpu.SemaphoreType.DMA,
            pltpu.SemaphoreType.DMA((piece_count,)),
            pltpu.SemaphoreType.DMA((piece_count,)),
            pltpu.SemaphoreType.DMA,
            pltpu.SemaphoreType.DMA,
            pltpu.SemaphoreType.DMA,
        ],
        compiler_params=pltpu.CompilerParams(
            collective_id=0, has_side_effects=True, vmem_limit_bytes=60 * 2**20
        ),
    )(
        cand_ids,
        cand_slot,
        *(
            vector.reshape(-1, LANES)
            for vector in (
                out_bias,
                norm1_gain,
                norm1_shift,
                up_bias,
                down_bias,
                norm2_gain,
                norm2_shift,
            )
        ),
        text_cache,
        images.transpose(1, 0, 2),
        w_key,
        w_value,
        w_query,
        w_out,
        w_up,
        w_down,
    )
    return pl.pallas_call(
        assemble,
        out_shape=jax.ShapeDtypeStruct((pair_count, word_count, width), BF16),
        in_specs=[anywhere],
        out_specs=anywhere,
        scratch_shapes=[
            pltpu.VMEM((dp_size, piece_count, group_rows, width), BF16),
            pltpu.VMEM((pair_count, word_count, width), BF16),
            pltpu.SemaphoreType.DMA((dp_size,)),
            pltpu.SemaphoreType.DMA((dp_size,)),
        ],
        compiler_params=pltpu.CompilerParams(vmem_limit_bytes=60 * 2**20),
    )(result)


def solution(mesh):
    split = P(("dp", "mem"), None, None)
    ids = P(("dp", "mem"), None)
    in_specs = (split, P("mem", None, None), ids, ids) + (P(),) * 13
    return jax.shard_map(
        on_device, mesh=mesh, in_specs=in_specs, out_specs=split, check_vma=False
    )
```
